256 devices in a mesh: sx: 32 (over y, z), sy: 8 (over x, core).
Axes of the slice: x: 4, y: 4, z: 8, core: 2. Of those that a mesh axis runs over, the one named last changes fastest.
Arguments:
- applied_loads: float32 [32, 8, 16, 192], P('sx', 'sy'), may hold values from -36 to 36
- bound_block: float32 [32, 8, 384, 384], P('sx', 'sy'), may hold values from -1 to 11, as said below
- coupling: float32 [32, 8, 384, 1152], P('sx', 'sy'), may hold values from -0.02 to 0.02
- interior_inverse: float32 [32, 8, 1152, 1152], P('sx', 'sy'), may hold values from -1 to 11, as said below
- local_inverse: float32 [32, 8, 384, 384], P('sx', 'sy'), may hold values from -1 to 11, as said below
- coarse_inverse: float32 [8192, 8192], P(('sx', 'sy')), may hold values from -1 to 11, as said below
Outputs:
- solution: float32 [32, 8, 16, 192], P('sx', 'sy')
- residual: float32 [32, 8, 16, 192], P('sx', 'sy')
- preconditioned: float32 [32, 8, 16, 192], P('sx', 'sy')
The draws below stay inside these ranges and needn't reach their ends.
Inputs may be any that keep to these rules, and one draw needn't show every extreme that they name: bound_block is symmetric in its last two dimensions. interior_inverse is symmetric in its last two dimensions. local_inverse is symmetric in its last two dimensions. coarse_inverse is symmetric.
All inputs are finite; a program needn't handle non-finite values.
Results may differ from the reference program's by a relative error of at most 0.0003.
Values sent between devices are 32-bit elements; how exact they have to be, the bound alone decides.
A program may use at most 64 MiB of HBM per device.

```python
import math
import jax
import jax.numpy as jnp
from jax import lax

F = 96
G = 16
NI = 1152
K = 16
ITERS = 2
NSX = 32
NSY = 8
NC = 8192


def symmetric_draw(key, leading, order, diagonal):
    uniform_part = jax.random.uniform(jax.random.fold_in(key, 11), leading + (order, order), jnp.float32, -1.0, 1.0)
    symmetric = (uniform_part + jnp.swapaxes(uniform_part, -1, -2)) * (0.7071 / math.sqrt(order))
    matrix = symmetric + diagonal * jnp.eye(order, dtype=jnp.float32)
    return matrix


def draw_applied_loads(key, part):
    rough = jnp.clip(jax.random.normal(jax.random.fold_in(key, 21), (NSX, NSY, K, 2 * F), jnp.float32), -4.0, 4.0)
    flat_index = jnp.arange(NSX * NSY).astype(jnp.float32).reshape(NSX, NSY)
    rising = 1.0 + 2.0 * flat_index / max(NSX * NSY - 1, 1)
    return rough * rising[:, :, None, None]


def draw_bound_block(key, part):
    return symmetric_draw(jax.random.fold_in(key, 31), (NSX, NSY), 4 * F, 2.5)


def draw_interior_inverse(key, part):
    return symmetric_draw(jax.random.fold_in(key, 41), (NSX, NSY), NI, 1.6)


def draw_local_inverse(key, part):
    return symmetric_draw(jax.random.fold_in(key, 51), (NSX, NSY), 4 * F, 1.5)


def draw_coarse_inverse(key, part):
    return symmetric_draw(jax.random.fold_in(key, 61), (), NC, 1.5)


def shard_levels(key, extent, shards, smallest, largest):
    def one(axis_at, parts):
        heights = jax.random.uniform(jax.random.fold_in(jax.random.fold_in(key, 6), axis_at), (parts,), jnp.float32, smallest / len(shards), largest / len(shards))
        return jnp.repeat(jnp.exp(heights), extent[axis_at] // parts).reshape((-1,) + (1,) * (len(extent) - axis_at - 1))

    factor_of = one(*shards[0])
    for cut in shards[1:]:
        factor_of = factor_of * one(*cut)
    return factor_of


def setup_inputs(seed: int = 0) -> dict:
    seeds = jax.random.split(jax.random.key(seed), 7)
    return {
        "applied_loads": draw_applied_loads(jax.random.fold_in(seeds[6], 71), 0),
        "bound_block": draw_bound_block(jax.random.fold_in(seeds[6], 71), 0),
        "coupling": jnp.clip(jax.random.uniform(seeds[2], (NSX, NSY, 4 * F, NI), jnp.float32, -0.02, 0.02) * shard_levels(seeds[2], (NSX, NSY, 4 * F, NI), ((0, 32), (1, 8)), -0.4, 0.0), -0.02, 0.02),
        "interior_inverse": draw_interior_inverse(jax.random.fold_in(seeds[6], 71), 0),
        "local_inverse": draw_local_inverse(jax.random.fold_in(seeds[6], 71), 0),
        "coarse_inverse": draw_coarse_inverse(jax.random.fold_in(seeds[6], 71), 0),
    }


precise = lax.Precision.HIGHEST


def local_faces(vector):
    east_face = vector[..., :F]
    south_face = vector[..., F:]
    west_face = jnp.concatenate([jnp.zeros_like(east_face[:, :1]), east_face[:, :-1]], axis=1)
    north_face = jnp.concatenate([jnp.zeros_like(south_face[:1]), south_face[:-1]], axis=0)
    return jnp.concatenate([west_face, east_face, north_face, south_face], axis=-1)


def assemble(result):
    from_west = result[..., :F]
    from_north = result[..., 2 * F:3 * F]
    east_total = result[..., F:2 * F] + jnp.concatenate([from_west[:, 1:], jnp.zeros_like(from_west[:, :1])], axis=1)
    south_total = result[..., 3 * F:] + jnp.concatenate([from_north[1:], jnp.zeros_like(from_north[:1])], axis=0)
    return jnp.concatenate([east_total, south_total], axis=-1)


def apply_schur(vector, bound_block, coupling, interior_inverse):
    faces = local_faces(vector)
    inner = jnp.einsum("abkf,abfi->abki", faces, coupling, precision=precise)
    solved = jnp.einsum("abki,abij->abkj", inner, interior_inverse, precision=precise)
    back = jnp.einsum("abkj,abfj->abkf", solved, coupling, precision=precise)
    first = jnp.einsum("abkf,abfg->abkg", faces, bound_block, precision=precise)
    return assemble(first - back)


def apply_precond(vector, local_inverse, coarse_inverse):
    faces = local_faces(vector)
    local_part = assemble(jnp.einsum("abkf,abfg->abkg", faces, local_inverse, precision=precise))
    run_length = F // G
    group_sums = vector.reshape(NSX, NSY, K, 2 * G, run_length).sum(axis=4)
    flat = jnp.transpose(group_sums, (2, 0, 1, 3)).reshape(K, NSX * NSY * 2 * G)
    correction = lax.dot_general(flat, coarse_inverse, (((1,), (1,)), ((), ())), precision=precise)
    spread = jnp.transpose(correction.reshape(K, NSX, NSY, 2 * G), (1, 2, 0, 3))
    return local_part + jnp.repeat(spread, run_length, axis=3)


def case_dot(left, right):
    return jnp.sum(left * right, axis=(0, 1, 3))


def reference(applied_loads, bound_block, coupling, interior_inverse, local_inverse, coarse_inverse):
    solution = jnp.zeros_like(applied_loads)
    residual = applied_loads
    preconditioned = apply_precond(residual, local_inverse, coarse_inverse)
    precond_dot = case_dot(residual, preconditioned)
    direction = preconditioned
    for step_index in range(ITERS):
        image_dir = apply_schur(direction, bound_block, coupling, interior_inverse)
        step_size = precond_dot / case_dot(direction, image_dir)
        solution = solution + step_size[:, None] * direction
        residual = residual - step_size[:, None] * image_dir
        preconditioned = apply_precond(residual, local_inverse, coarse_inverse)
        if step_index + 1 < ITERS:
            next_dot = case_dot(residual, preconditioned)
            direction = preconditioned + (next_dot / precond_dot)[:, None] * direction
            precond_dot = next_dot
    return (solution, residual, preconditioned)
```

```python
import jax
import jax.numpy as jnp
from jax import lax
from jax.experimental import pallas as pl
from jax.experimental.pallas import tpu as pltpu
from jax.sharding import PartitionSpec as P

MESH = pl.DeviceIdType.MESH
F = 96
FP = 128
FACES = 4
K = 16
NF = FACES * F
NP = FACES * FP
NI = 1152
NC = 8192
LX, LY, LZ = 4, 4, 8
COLS = 384
f32, bf16 = jnp.float32, jnp.bfloat16

LOADS_W, LOADS_N = 0, 1
PRE0, PRE1, PRE2 = 2, 4, 6
Z0, Z1 = 8, 10
SCH0, SCH1 = 12, 16
SLOTS = 20


def split(value):
    high = value.astype(bf16)
    low = (value - high.astype(f32)).astype(bf16)
    return high, low


def dot(left, right):
    return jnp.dot(left, right, preferred_element_type=f32)


def dot_t(left, right):
    return lax.dot_general(left, right, (((1,), (1,)), ((), ())), preferred_element_type=f32)


def pad_split(get_block, high_ref, low_ref):
    high_ref[...] = jnp.zeros_like(high_ref)
    low_ref[...] = jnp.zeros_like(low_ref)
    for a in range(FACES):
        for b in range(FACES):
            high, low = split(get_block(a, b))
            high_ref[a * FP : a * FP + F, b * FP : b * FP + F] = high
            low_ref[a * FP : a * FP + F, b * FP : b * FP + F] = low


def apply_local(faces, high_ref, low_ref):
    high, low = split(jnp.concatenate(faces, axis=1))
    both = dot(jnp.concatenate([high, low], axis=0), high_ref[...])
    result = both[:K] + both[K:] + dot(high, low_ref[...])
    return [result[:, f * FP : (f + 1) * FP] for f in range(FACES)]


def kernel(
    loads_ref, bound_ref, coupling_ref, interior_ref, local_ref, coarse_ref,
    x_ref, r_ref, z_ref,
    loads_v, bound_v, coupling_v, interior_v, local_v, coarse_v, load_sem,
    l_high, l_low, s_high, s_low, c_high, c_low, i_high, i_low, t_high, t_low, schur_v,
    permuted, partner_rows, coarse_w,
    line_v, plane_v, part_out, part_in, halo_out, halo_in,
    line_send, line_recv, plane_send, plane_recv, swap_send, swap_recv, part_send, part_recv, halo_send, halo_recv,
):
    i = lax.axis_index("sx")
    j = lax.axis_index("sy")
    y, z = lax.div(i, LZ), lax.rem(i, LZ)
    x, core = lax.div(j, 2), lax.rem(j, 2)
    block = y * LX + x
    east = {"sx": i, "sy": lax.rem(j + 1, 2 * LX)}
    west = {"sx": i, "sy": lax.rem(j + 2 * LX - 1, 2 * LX)}
    south = {"sx": lax.rem(i + 1, LY * LZ), "sy": j}
    north = {"sx": lax.rem(i + LY * LZ - 1, LY * LZ), "sy": j}
    partner = {"sx": i, "sy": x * 2 + (1 - core)}
    line = [{"sx": y * LZ + lax.rem(z + s, LZ), "sy": j} for s in range(1, LZ)]
    plane = [
        {"sx": lax.rem(y + s // LX, LY) * LZ + z, "sy": lax.rem(x + s % LX, LX) * 2 + core} for s in range(1, LX * LY)
    ]

    barrier = pltpu.get_barrier_semaphore()
    greeted = [east, west, south, north, partner] + line + plane
    for device in greeted:
        pl.semaphore_signal(barrier, 1, device_id=device, device_id_type=MESH)

    fetches = [
        pltpu.make_async_copy(source, target, load_sem.at[k])
        for k, (source, target) in enumerate(
            [
                (loads_ref.at[0, 0], loads_v),
                (coarse_ref, coarse_v),
                (local_ref.at[0, 0], local_v),
                (coupling_ref.at[0, 0], coupling_v),
                (interior_ref.at[0, 0], interior_v),
                (bound_ref.at[0, 0], bound_v),
            ]
        )
    ]
    for fetch in fetches:
        fetch.start()

    has_west, has_east = j > 0, j < 2 * LX - 1
    has_north, has_south = i > 0, i < LY * LZ - 1

    def halo_copy(slot, device):
        return pltpu.make_async_remote_copy(
            halo_out.at[slot], halo_in.at[slot], halo_send.at[slot], halo_recv.at[slot], device_id=device, device_id_type=MESH
        )

    def halo_start(slot, device, value):
        halo_out[slot] = value
        copy = halo_copy(slot, device)
        copy.start()
        started.append(copy)

    def halo_wait(slot, device, present):
        halo_copy(slot, device).wait_recv()
        return jnp.where(present, halo_in[slot], 0.0)

    started = []

    lane_row = lax.broadcasted_iota(jnp.int32, (1, FP), 1)
    lane_group = lane_row // 32
    value_lane = lax.broadcasted_iota(jnp.int32, (2 * FP, FP), 0)
    coarse_lane = lax.broadcasted_iota(jnp.int32, (2 * FP, FP), 1) % 32
    in_face = value_lane % FP
    run_of = (value_lane // FP) * 16 + in_face // 6
    restrict = ((run_of == coarse_lane) & (in_face < F)).astype(f32).astype(bf16)
    coarse_at = lax.broadcasted_iota(jnp.int32, (FP, 2 * FP), 0)
    value_at = lax.broadcasted_iota(jnp.int32, (FP, 2 * FP), 1)
    value_in = value_at % FP
    spread_of = (value_at // FP) * 16 + value_in // 6
    spread = ((spread_of == coarse_at % 64) & (value_in < F)).astype(f32).astype(bf16)

    def line_copy(phase, s):
        return pltpu.make_async_remote_copy(
            line_v.at[phase, z], line_v.at[phase, z], line_send.at[phase, s], line_recv.at[phase, s],
            device_id=line[s - 1], device_id_type=MESH,
        )

    def plane_copy(phase, s):
        return pltpu.make_async_remote_copy(
            plane_v.at[phase, block], plane_v.at[phase, block], plane_send.at[phase, s], plane_recv.at[phase, s],
            device_id=plane[s - 1], device_id_type=MESH,
        )

    def part_copy(phase):
        return pltpu.make_async_remote_copy(
            part_out.at[phase], part_in.at[phase], part_send.at[phase], part_recv.at[phase],
            device_id=partner, device_id_type=MESH,
        )

    def gather_prepare(phase, east_face, south_face, dots):
        value = jnp.concatenate([east_face, south_face], axis=1)
        high, rest = value.astype(bf16), None
        rest = value - high.astype(f32)
        middle, low = split(rest)
        sums = dot(jnp.concatenate([high, middle, low], axis=0), restrict)
        sums = sums[:K] + sums[K : 2 * K] + sums[2 * K :]
        packed = jnp.zeros((4, FP), f32)
        for q in range(4):
            packed = jnp.where(lane_group == q, sums[4 * q : 4 * q + 4], packed)
        placed = jnp.zeros((K, FP), f32)
        case = lax.broadcasted_iota(jnp.int32, (K, FP), 0)
        lane = lax.broadcasted_iota(jnp.int32, (K, FP), 1)
        for d, (left, right) in enumerate(dots):
            product = left[0] * right[0] + left[1] * right[1]
            placed = jnp.where(lane == d * K + case, jnp.sum(product, axis=1, keepdims=True), placed)
        row = jnp.sum(placed, axis=0, keepdims=True)
        line_v[phase, z] = jnp.concatenate([packed, jnp.broadcast_to(row, (4, FP))], axis=0)

    def gather_start(phase):
        for s in range(1, LZ):
            copy = line_copy(phase, s)
            copy.start()
            started.append(copy)

    def gather_forward(phase):
        for s in range(1, LZ):
            line_copy(phase, s).wait_recv()
        tiles = [line_v[phase, s] for s in range(LZ)]
        for h in range(2):
            rows = []
            for q in range(4):
                mixed = jnp.zeros((8, FP), f32)
                for d in range(4):
                    turn = ((d - q) % 4) * 32
                    tile = tiles[4 * h + d]
                    turned = pltpu.roll(tile, turn, 1) if turn else tile
                    mixed = jnp.where(lane_group == d, turned, mixed)
                rows.append(mixed[:4])
            plane_v[phase, block, h * K : (h + 1) * K] = jnp.concatenate(rows, axis=0)
        total = tiles[0]
        for s in range(1, LZ):
            total = total + tiles[s]
        plane_v[phase, block, 2 * K :] = total
        for s in range(1, LX * LY):
            copy = plane_copy(phase, s)
            copy.start()
            started.append(copy)

    def gather_finish(phase):
        for s in range(1, LX * LY):
            plane_copy(phase, s).wait_recv()
        total = jnp.zeros((2 * K, FP), f32)
        sums = jnp.zeros((8, FP), f32)
        for b in range(LX * LY):
            value = jnp.concatenate([plane_v[phase, b, :K], plane_v[phase, b, K : 2 * K]], axis=1)
            high, low = split(value)
            total += dot_t(jnp.concatenate([high, low], axis=0), coarse_w[:, b * 256 : (b + 1) * 256])
            sums += plane_v[phase, b, 2 * K :]
        part = total[:K] + total[K:]
        part_out[phase, :K] = part
        part_out[phase, K:] = sums
        copy = part_copy(phase)
        copy.start()
        started.append(copy)
        part_copy(phase).wait_recv()
        own = part + pltpu.roll(part_in[phase, :K], FP - 32, 1)
        sums = sums + part_in[phase, K:]
        high, low = split(own)
        wide = dot(jnp.concatenate([high, low], axis=0), spread)
        wide = wide[:K] + wide[K:]
        case = lax.broadcasted_iota(jnp.int32, (K, FP), 0)
        lane = lax.broadcasted_iota(jnp.int32, (K, FP), 1)

        def column(d):
            return jnp.sum(jnp.where(lane == d * K + case, sums[4:5], 0.0), axis=1, keepdims=True)

        return wide[:, :FP], wide[:, FP:], column

    def precond_local(phase, slot, faces):
        result = apply_local(faces, l_high, l_low)
        halo_start(slot, west, result[0])
        halo_start(slot + 1, north, result[2])
        return result[1], result[3]

    def precond_finish(phase, slot, mine):
        add_east = halo_wait(slot, west, has_east)
        add_south = halo_wait(slot + 1, north, has_south)
        wide_east, wide_south, column = gather_finish(phase)
        return mine[0] + add_east + wide_east, mine[1] + add_south + wide_south, column

    def share_faces(slot, value):
        halo_start(slot, east, value[0])
        halo_start(slot + 1, south, value[1])
        from_west = halo_wait(slot, east, has_west)
        from_north = halo_wait(slot + 1, south, has_north)
        return [from_west, value[0], from_north, value[1]]

    def schur(slot, faces):
        result = apply_local(faces, s_high, s_low)
        halo_start(slot, west, result[0])
        halo_start(slot + 1, north, result[2])
        halo_start(slot + 2, east, result[1])
        halo_start(slot + 3, south, result[3])
        east_total = result[1] + halo_wait(slot, west, has_east)
        south_total = result[3] + halo_wait(slot + 1, north, has_south)
        west_total = jnp.where(has_west, result[0] + halo_wait(slot + 2, east, has_west), 0.0)
        north_total = jnp.where(has_north, result[2] + halo_wait(slot + 3, south, has_north), 0.0)
        return [west_total, east_total, north_total, south_total]

    fetches[0].wait()
    padding = jnp.zeros((K, FP - F), f32)
    r0 = (
        jnp.concatenate([loads_v[:, :F], padding], axis=1),
        jnp.concatenate([loads_v[:, F : 2 * F], padding], axis=1),
    )
    gather_prepare(0, r0[0], r0[1], [])
    pl.semaphore_wait(barrier, len(greeted))
    gather_start(0)
    halo_start(LOADS_W, east, r0[0])
    halo_start(LOADS_N, south, r0[1])

    fetches[1].wait()

    def permute(step, _):
        y_at, rest = lax.div(step, 4), lax.rem(step, 4)
        half, j_half = lax.div(rest, 2), lax.rem(rest, 2)
        tiles = []
        for d in range(4):
            at = ((y_at * LZ + half * 4 + d) * 2 + j_half) * FP
            tiles.append(coarse_v[:, pl.ds(pl.multiple_of(at, FP), FP)])
        for q in range(4):
            mixed = tiles[q] if q == 0 else pltpu.roll(tiles[0], ((0 - q) % 4) * 32, 1)
            for d in range(1, 4):
                turn = ((d - q) % 4) * 32
                turned = pltpu.roll(tiles[d], turn, 1) if turn else tiles[d]
                mixed = jnp.where(lane_group == d, turned, mixed)
            at = (y_at * LX + j_half * 2 + q // 2) * 256 + half * FP
            permuted[q % 2, :, pl.ds(pl.multiple_of(at, FP), FP)] = mixed
        return 0

    lax.fori_loop(0, 16, permute, 0)
    swap = pltpu.make_async_remote_copy(
        permuted.at[1 - core], partner_rows, swap_send, swap_recv, device_id=partner, device_id_type=MESH
    )
    swap.start()
    started.append(swap)

    fetches[2].wait()
    pad_split(lambda a, b: local_v[a * F : (a + 1) * F, b * F : (b + 1) * F], l_high, l_low)
    from_west = halo_wait(LOADS_W, east, has_west)
    from_north = halo_wait(LOADS_N, south, has_north)
    mine = precond_local(0, PRE0, [from_west, r0[0], from_north, r0[1]])

    gather_forward(0)

    high, low = split(permuted[core])
    coarse_w[0:32], coarse_w[64:96] = high, low
    swap.wait_recv()
    high, low = split(partner_rows[...])
    coarse_w[32:64], coarse_w[96:128] = high, low

    fetches[3].wait()
    c_high[...], c_low[...] = split(coupling_v[...])
    fetches[4].wait()

    def times_interior(step, _):
        columns = pl.ds(pl.multiple_of(step * COLS, FP), COLS)
        i_high[...], i_low[...] = split(interior_v[:, columns])
        total = dot(c_high[...], i_high[...]) + dot(c_low[...], i_high[...]) + dot(c_high[...], i_low[...])
        t_high[:, columns], t_low[:, columns] = split(total)
        return 0

    lax.fori_loop(0, NI // COLS, times_interior, 0)
    back = dot_t(t_high[...], c_high[...]) + dot_t(t_low[...], c_high[...]) + dot_t(t_high[...], c_low[...])
    fetches[5].wait()
    schur_v[...] = bound_v[...] - back
    pad_split(lambda a, b: schur_v[a * F : (a + 1) * F, b * F : (b + 1) * F], s_high, s_low)

    z0_east, z0_south, _ = precond_finish(0, PRE0, mine)
    z0 = (z0_east, z0_south)

    q0_faces = schur(SCH0, share_faces(Z0, z0))
    q0 = (q0_faces[1], q0_faces[3])
    gather_prepare(1, q0[0], q0[1], [(r0, z0), (z0, q0)])
    gather_start(1)
    mine = precond_local(1, PRE1, q0_faces)
    gather_forward(1)
    w0_east, w0_south, column = precond_finish(1, PRE1, mine)
    w0 = (w0_east, w0_south)
    rz0, dq0 = column(0), column(1)
    step0 = rz0 / dq0
    z1 = tuple(a - step0 * b for a, b in zip(z0, w0))

    z1_faces = share_faces(Z1, z1)
    r1 = tuple(a - step0 * b for a, b in zip(r0, q0))
    t1_faces = schur(SCH1, z1_faces)
    t1 = (t1_faces[1], t1_faces[3])
    gather_prepare(2, t1[0], t1[1], [(r1, z1), (z1, t1), (z0, t1), (z1, q0)])
    gather_start(2)
    mine = precond_local(2, PRE2, t1_faces)
    gather_forward(2)
    w1_east, w1_south, column = precond_finish(2, PRE2, mine)
    w1 = (w1_east, w1_south)

    rz1 = column(0)
    ratio = rz1 / rz0
    step1 = rz1 / (column(1) + ratio * (column(2) + column(3)) + ratio * ratio * dq0)
    for f in range(2):
        place = slice(f * F, (f + 1) * F)
        direction = z1[f] + ratio * z0[f]
        x_ref[0, 0, :, place] = (step0 * z0[f] + step1 * direction)[:, :F]
        r_ref[0, 0, :, place] = (r1[f] - step1 * (t1[f] + ratio * q0[f]))[:, :F]
        z_ref[0, 0, :, place] = (z1[f] - step1 * (w1[f] + ratio * w0[f]))[:, :F]

    for copy in started:
        copy.wait_send()


def shards(applied_loads, bound_block, coupling, interior_inverse, local_inverse, coarse_inverse):
    out = jax.ShapeDtypeStruct((1, 1, K, 2 * F), f32)
    dma = pltpu.SemaphoreType.DMA
    return pl.pallas_call(
        kernel,
        out_shape=(out, out, out),
        in_specs=[pl.BlockSpec(memory_space=pl.ANY)] * 6,
        out_specs=tuple(pl.BlockSpec(memory_space=pltpu.VMEM) for _ in range(3)),
        scratch_shapes=[
            pltpu.VMEM((K, 2 * F), f32),
            pltpu.VMEM((NF, NF), f32),
            pltpu.VMEM((NF, NI), f32),
            pltpu.VMEM((NI, NI), f32),
            pltpu.VMEM((NF, NF), f32),
            pltpu.VMEM((32, NC), f32),
            dma((6,)),
            pltpu.VMEM((NP, NP), bf16),
            pltpu.VMEM((NP, NP), bf16),
            pltpu.VMEM((NP, NP), bf16),
            pltpu.VMEM((NP, NP), bf16),
            pltpu.VMEM((NF, NI), bf16),
            pltpu.VMEM((NF, NI), bf16),
            pltpu.VMEM((NI, COLS), bf16),
            pltpu.VMEM((NI, COLS), bf16),
            pltpu.VMEM((NF, NI), bf16),
            pltpu.VMEM((NF, NI), bf16),
            pltpu.VMEM((NF, NF), f32),
            pltpu.VMEM((2, 32, NC // 2), f32),
            pltpu.VMEM((32, NC // 2), f32),
            pltpu.VMEM((128, NC // 2), bf16),
            pltpu.VMEM((3, LZ, 8, FP), f32),
            pltpu.VMEM((3, LX * LY, 40, FP), f32),
            pltpu.VMEM((3, 24, FP), f32),
            pltpu.VMEM((3, 24, FP), f32),
            pltpu.VMEM((SLOTS, K, FP), f32),
            pltpu.VMEM((SLOTS, K, FP), f32),
            dma((3, LZ)),
            dma((3, LZ)),
            dma((3, LX * LY)),
            dma((3, LX * LY)),
            dma,
            dma,
            dma((3,)),
            dma((3,)),
            dma((SLOTS,)),
            dma((SLOTS,)),
        ],
        compiler_params=pltpu.CompilerParams(
            collective_id=0, has_side_effects=True, vmem_limit_bytes=40 * 1024 * 1024
        ),
    )(applied_loads, bound_block, coupling, interior_inverse, local_inverse, coarse_inverse)


def solution(mesh):
    blocks = P("sx", "sy", None, None)
    return jax.shard_map(
        shards,
        mesh=mesh,
        in_specs=(blocks, blocks, blocks, blocks, blocks, P(("sx", "sy"), None)),
        out_specs=(blocks, blocks, blocks),
        check_vma=False,
    )
```

```python
import jax
import jax.numpy as jnp
from jax import lax
from jax.experimental import pallas as pl
from jax.experimental.pallas import tpu as pltpu
from jax.sharding import PartitionSpec as P

MESH = pl.DeviceIdType.MESH
F = 96
FP = 128
FACES = 4
K = 16
NF = FACES * F
NP = FACES * FP
NI = 1152
NC = 8192
LX, LY, LZ = 4, 4, 8
COLS = 384
PLANE_ORDER = sorted(range(LX * LY), key=lambda s: min(s // LX, LY - s // LX) + min(s % LX, LX - s % LX))
f32, bf16 = jnp.float32, jnp.bfloat16

LOADS_W, LOADS_N = 0, 1
PRE0, PRE1, PRE2 = 2, 6, 10
SCH0, SCH1 = 12, 16
SLOTS = 20


def split(value):
    high = value.astype(bf16)
    low = (value - high.astype(f32)).astype(bf16)
    return high, low


def dot(left, right):
    return jnp.dot(left, right, preferred_element_type=f32)


def dot_t(left, right):
    return lax.dot_general(left, right, (((1,), (1,)), ((), ())), preferred_element_type=f32)


def pad_split(get_block, high_ref, low_ref):
    high_ref[...] = jnp.zeros_like(high_ref)
    low_ref[...] = jnp.zeros_like(low_ref)
    for a in range(FACES):
        for b in range(FACES):
            high, low = split(get_block(a, b))
            high_ref[a * FP : a * FP + F, b * FP : b * FP + F] = high
            low_ref[a * FP : a * FP + F, b * FP : b * FP + F] = low


def apply_local(faces, high_ref, low_ref):
    high, low = split(jnp.concatenate(faces, axis=1))
    both = dot(jnp.concatenate([high, low], axis=0), high_ref[...])
    result = both[:K] + both[K:] + dot(high, low_ref[...])
    return [result[:, f * FP : (f + 1) * FP] for f in range(FACES)]


def kernel(
    loads_ref, bound_ref, coupling_ref, interior_ref, local_ref, coarse_ref,
    out_ref,
    loads_v, bound_v, coupling_v, interior_v, local_v, coarse_v, load_sem,
    l_high, l_low, s_high, s_low, c_high, c_low, i_high, i_low, t_high, t_low, schur_v,
    permuted, partner_rows, coarse_w, restrict_v, spread_v,
    line_v, west_out, west_in, head_in, plane_v, part_out, part_in, halo_out, halo_in,
    line_send, line_recv, west_send, west_recv, head_send, head_recv, plane_send, plane_recv,
    swap_send, swap_recv, part_send, part_recv, halo_send, halo_recv,
):
    i = lax.axis_index("sx")
    j = lax.axis_index("sy")
    y, z = lax.div(i, LZ), lax.rem(i, LZ)
    x, core = lax.div(j, 2), lax.rem(j, 2)
    block = y * LX + x
    east = {"sx": i, "sy": lax.rem(j + 1, 2 * LX)}
    west = {"sx": i, "sy": lax.rem(j + 2 * LX - 1, 2 * LX)}
    south = {"sx": lax.rem(i + 1, LY * LZ), "sy": j}
    north = {"sx": lax.rem(i + LY * LZ - 1, LY * LZ), "sy": j}
    partner = {"sx": i, "sy": x * 2 + (1 - core)}
    line = [{"sx": y * LZ + lax.rem(z + s, LZ), "sy": j} for s in range(LZ)]
    west_line = [{"sx": device["sx"], "sy": west["sy"]} for device in line]
    east_line = [{"sx": device["sx"], "sy": east["sy"]} for device in line]
    north_line = [{"sx": lax.rem(y + LY - 1, LY) * LZ + s, "sy": j} for s in range(LZ)]
    south_head = {"sx": lax.rem(y + 1, LY) * LZ, "sy": j}
    plane = [
        {"sx": lax.rem(y + s // LX, LY) * LZ + z, "sy": lax.rem(x + s % LX, LX) * 2 + core} for s in range(LX * LY)
    ]
    south_pair = [south, {"sx": south["sx"], "sy": partner["sy"]}]
    east_pair = [{"sx": i, "sy": lax.rem(x + 1, LX) * 2 + core}, {"sx": i, "sy": lax.rem(x + 1, LX) * 2 + 1 - core}]
    north_other = {"sx": north["sx"], "sy": partner["sy"]}
    west_other = {"sx": i, "sy": lax.rem(x + LX - 1, LX) * 2 + 1 - core}

    barrier = pltpu.get_barrier_semaphore()
    greeted = [east, west, south, north, partner, north_other, west_other, south_head]
    greeted += line[1:] + plane[1:] + east_line
    for device in greeted:
        pl.semaphore_signal(barrier, 1, device_id=device, device_id_type=MESH)

    fetches = [
        pltpu.make_async_copy(source, target, load_sem.at[k])
        for k, (source, target) in enumerate(
            [
                (loads_ref.at[0, 0], loads_v),
                (coarse_ref, coarse_v),
                (coupling_ref.at[0, 0], coupling_v),
                (interior_ref.at[0, 0], interior_v),
                (local_ref.at[0, 0], local_v),
                (bound_ref.at[0, 0], bound_v),
            ]
        )
    ]
    for fetch in fetches:
        fetch.start()

    has_west, has_east = j > 0, j < 2 * LX - 1
    has_north, has_south = i > 0, i < LY * LZ - 1

    def halo_copy(slot, device):
        return pltpu.make_async_remote_copy(
            halo_out.at[slot], halo_in.at[slot], halo_send.at[slot], halo_recv.at[slot], device_id=device, device_id_type=MESH
        )

    def halo_start(slot, device, value):
        halo_out[slot] = value
        copy = halo_copy(slot, device)
        copy.start()
        started.append(copy)

    def halo_wait(slot, device, present):
        halo_copy(slot, device).wait_recv()
        return jnp.where(present, halo_in[slot], 0.0)

    started = []

    lane_row = lax.broadcasted_iota(jnp.int32, (1, FP), 1)
    lane_group = lane_row // 32
    south_lanes = lane_row % 32 >= 16
    case = lax.broadcasted_iota(jnp.int32, (K, FP), 0)
    lane = lax.broadcasted_iota(jnp.int32, (K, FP), 1)
    value_lane = lax.broadcasted_iota(jnp.int32, (2 * FP, FP), 0)
    coarse_lane = lax.broadcasted_iota(jnp.int32, (2 * FP, FP), 1) % 32
    in_face = value_lane % FP
    run_of = (value_lane // FP) * 16 + in_face // 6
    restrict_v[...] = ((run_of == coarse_lane) & (in_face < F)).astype(f32).astype(bf16)
    coarse_at = lax.broadcasted_iota(jnp.int32, (FP, 3 * FP), 0) % 64
    value_at = lax.broadcasted_iota(jnp.int32, (FP, 3 * FP), 1)
    value_in = value_at % FP
    face_at = value_at // FP
    first = jnp.where(face_at == 2, (1 - core) * 32, core * 32 + face_at * 16)
    spread_v[...] = ((first + value_in // 6 == coarse_at) & (value_in < F)).astype(f32).astype(bf16)

    def line_copy(phase, s):
        return pltpu.make_async_remote_copy(
            line_v.at[phase, z], line_v.at[phase, z], line_send.at[phase, s], line_recv.at[phase, s],
            device_id=line[s], device_id_type=MESH,
        )

    def west_copy(phase, s):
        return pltpu.make_async_remote_copy(
            west_out.at[phase], west_in.at[phase, z], west_send.at[phase, s], west_recv.at[phase, s],
            device_id=west_line[s], device_id_type=MESH,
        )

    def head_copy(phase, s):
        return pltpu.make_async_remote_copy(
            line_v.at[phase, z], head_in.at[phase], head_send.at[phase, s], head_recv.at[phase],
            device_id=north_line[s], device_id_type=MESH,
        )

    def plane_copy(phase, s):
        return pltpu.make_async_remote_copy(
            plane_v.at[phase, block], plane_v.at[phase, block], plane_send.at[phase, s], plane_recv.at[phase, s],
            device_id=plane[s], device_id_type=MESH,
        )

    def part_copy(phase, k, slot, device):
        return pltpu.make_async_remote_copy(
            part_out.at[phase], part_in.at[phase, slot], part_send.at[phase, k], part_recv.at[phase, slot],
            device_id=device, device_id_type=MESH,
        )

    def go(copy):
        copy.start()
        started.append(copy)

    def pack(sums):
        packed = sums[:4]
        for q in range(1, 4):
            packed = jnp.where(lane_group == q, sums[4 * q : 4 * q + 4], packed)
        return packed

    def gather_start(phase, own, shared, dots):
        values = [jnp.concatenate(own, axis=1)] + ([jnp.concatenate(shared, axis=1)] if shared else [])
        high, low = split(jnp.concatenate(values, axis=0))
        rows = len(values) * K
        sums = dot(jnp.concatenate([high, low], axis=0), restrict_v[...])
        sums = sums[:rows] + sums[rows:]
        line_v[phase, z, :4] = pack(sums[:K])
        if not shared:
            line_v[phase, z, 4:] = jnp.zeros((4, FP), f32)
        else:
            others = pack(sums[K:])
            west_out[phase] = others
            for s in range(LZ):
                go(west_copy(phase, s))
            placed = jnp.zeros((K, FP), f32)
            for d, (left, right) in enumerate(dots):
                product = left[0] * right[0]
                for f in range(1, len(left)):
                    product += left[f] * right[f]
                placed = jnp.where(lane == d * 32 + case, jnp.sum(product, axis=1, keepdims=True), placed)
            row = jnp.sum(placed, axis=0, keepdims=True)
            line_v[phase, z, 4:] = jnp.where(south_lanes, others, row)

            @pl.when(z == 0)
            def _():
                for s in range(LZ):
                    head_copy(phase, s).start()

        for s in range(1, LZ):
            go(line_copy(phase, s))

    def gather_forward(phase, shared):
        for s in range(1, LZ):
            line_copy(phase, s).wait_recv()
        if shared:
            for s in range(LZ):
                west_copy(phase, s).wait_recv()
            head_copy(phase, 0).wait_recv()
        tiles = []
        for s in range(LZ):
            tile = line_v[phase, s, :4]
            if shared:
                if s + 1 < LZ:
                    below = line_v[phase, s + 1, 4:]
                else:
                    below = jnp.where(y < LY - 1, head_in[phase, 4:], 0.0)
                right = jnp.where(has_east, west_in[phase, s], 0.0)
                tile = tile + jnp.where(south_lanes, below, right)
            tiles.append(tile)
        for h in range(2):
            rows = []
            for q in range(4):
                mixed = None
                for d in range(4):
                    turn = ((d - q) % 4) * 32
                    tile = tiles[4 * h + d]
                    turned = pltpu.roll(tile, turn, 1) if turn else tile
                    mixed = turned if mixed is None else jnp.where(lane_group == d, turned, mixed)
                rows.append(mixed)
            plane_v[phase, block, h * K : (h + 1) * K] = jnp.concatenate(rows, axis=0)
        total = line_v[phase, 0]
        for s in range(1, LZ):
            total = total + line_v[phase, s]
        plane_v[phase, block, 2 * K :] = total
        for s in PLANE_ORDER[1:]:
            go(plane_copy(phase, s))

    def gather_finish(phase, last):
        total = jnp.zeros((2 * K, FP), f32)
        sums = jnp.zeros((8, FP), f32)
        for s in PLANE_ORDER:
            if s:
                plane_copy(phase, s).wait_recv()
            b = lax.rem(y + LY - s // LX, LY) * LX + lax.rem(x + LX - s % LX, LX)
            value = jnp.concatenate([plane_v[phase, b, :K], plane_v[phase, b, K : 2 * K]], axis=1)
            high, low = split(value)
            total += dot_t(jnp.concatenate([high, low], axis=0), coarse_w[b])
            sums += plane_v[phase, b, 2 * K :]
        part = total[:K] + total[K:]
        part_out[phase, :K] = part
        part_out[phase, K:] = sums
        if not last:
            for k in range(2):
                go(part_copy(phase, k, 1 + core, south_pair[k]))
                go(part_copy(phase, 2 + k, 3 + core, east_pair[k]))
        go(part_copy(phase, 4, 0, partner))
        part_copy(phase, 4, 0, partner).wait_recv()
        own = part + part_in[phase, 0, :K]
        sums = sums + part_in[phase, 0, K:]

        def column(d):
            return jnp.sum(jnp.where(lane == d * 32 + case, sums[4:5], 0.0), axis=1, keepdims=True)

        groups = [own]
        if not last:
            for slot in range(1, 5):
                part_copy(phase, 0, slot, partner).wait_recv()
            groups.append(part_in[phase, 1, :K] + part_in[phase, 2, :K])
            groups.append(jnp.where(core == 0, part_in[phase, 3, :K] + part_in[phase, 4, :K], own))
        high, low = split(jnp.concatenate(groups, axis=0))
        rows = len(groups) * K
        wide = dot(jnp.concatenate([high, low], axis=0), spread_v[...])
        wide = wide[:rows] + wide[rows:]
        faces = [wide[:K, :FP], wide[:K, FP : 2 * FP]]
        if not last:
            faces = [wide[2 * K :, 2 * FP :], faces[0], wide[K : 2 * K, FP : 2 * FP], faces[1]]
        return faces, column

    def spread_faces(slot, result, last=False):
        halo_start(slot, west, result[0])
        halo_start(slot + 1, north, result[2])
        if not last:
            halo_start(slot + 2, east, result[1])
            halo_start(slot + 3, south, result[3])

    def total_faces(slot, result, last=False):
        east_total = result[1] + halo_wait(slot, west, has_east)
        south_total = result[3] + halo_wait(slot + 1, north, has_south)
        if last:
            return [east_total, south_total]
        west_total = result[0] + halo_wait(slot + 2, east, has_west)
        north_total = result[2] + halo_wait(slot + 3, south, has_north)
        return inner_faces([west_total, east_total, north_total, south_total])

    def inner_faces(faces):
        return [jnp.where(has_west, faces[0], 0.0), faces[1], jnp.where(has_north, faces[2], 0.0), faces[3]]

    def owned(faces):
        return [faces[1], faces[3]]

    fetches[0].wait()
    padding = jnp.zeros((K, FP - F), f32)
    r0 = [
        jnp.concatenate([loads_v[:, :F], padding], axis=1),
        jnp.concatenate([loads_v[:, F : 2 * F], padding], axis=1),
    ]

    fetches[1].wait()

    def permute(step, _):
        y_at, rest = lax.div(step, 4), lax.rem(step, 4)
        half, j_half = lax.div(rest, 2), lax.rem(rest, 2)
        tiles = []
        for d in range(4):
            at = ((y_at * LZ + half * 4 + d) * 2 + j_half) * FP
            tiles.append(coarse_v[:, pl.ds(pl.multiple_of(at, FP), FP)])
        for q in range(4):
            mixed = tiles[q] if q == 0 else pltpu.roll(tiles[0], ((0 - q) % 4) * 32, 1)
            for d in range(1, 4):
                turn = ((d - q) % 4) * 32
                turned = pltpu.roll(tiles[d], turn, 1) if turn else tiles[d]
                mixed = jnp.where(lane_group == d, turned, mixed)
            at = (y_at * LX + j_half * 2 + q // 2) * 256 + half * FP
            permuted[q % 2, :, pl.ds(pl.multiple_of(at, FP), FP)] = mixed
        return 0

    lax.fori_loop(0, 16, permute, 0)
    fetches[2].wait()
    c_high[...], c_low[...] = split(coupling_v[...])

    pl.semaphore_wait(barrier, len(greeted) - 1 + LZ * lax.div(LZ - 1 - z, LZ - 1))

    gather_start(0, r0, None, None)
    halo_start(LOADS_W, east, r0[0])
    halo_start(LOADS_N, south, r0[1])
    swap = pltpu.make_async_remote_copy(
        permuted.at[1 - core], partner_rows, swap_send, swap_recv, device_id=partner, device_id_type=MESH
    )
    go(swap)

    def times_interior(step, _):
        columns = pl.ds(pl.multiple_of(step * COLS, FP), COLS)
        i_high[...], i_low[...] = split(interior_v[:, columns])
        total = dot(c_high[...], i_high[...]) + dot(c_low[...], i_high[...]) + dot(c_high[...], i_low[...])
        t_high[:, columns], t_low[:, columns] = split(total)
        return 0

    fetches[3].wait()
    lax.fori_loop(0, 1, times_interior, 0)

    fetches[4].wait()
    pad_split(lambda a, b: local_v[a * F : (a + 1) * F, b * F : (b + 1) * F], l_high, l_low)
    from_west = halo_wait(LOADS_W, east, has_west)
    from_north = halo_wait(LOADS_N, south, has_north)
    z0_local = apply_local([from_west, r0[0], from_north, r0[1]], l_high, l_low)
    spread_faces(PRE0, z0_local)

    gather_forward(0, False)

    def place_rows(value, at):
        high, low = split(value)
        for b in range(LX * LY):
            coarse_w[b, pl.ds(pl.multiple_of(at, 32), 32)] = high[:, b * 256 : (b + 1) * 256]
            coarse_w[b, pl.ds(pl.multiple_of(64 + at, 32), 32)] = low[:, b * 256 : (b + 1) * 256]

    place_rows(permuted[core], core * 32)
    swap.wait_recv()
    place_rows(partner_rows[...], (1 - core) * 32)
    lax.fori_loop(1, NI // COLS, times_interior, 0)
    back = dot_t(t_high[...], c_high[...]) + dot_t(t_low[...], c_high[...]) + dot_t(t_high[...], c_low[...])
    fetches[5].wait()
    schur_v[...] = bound_v[...] - back
    pad_split(lambda a, b: schur_v[a * F : (a + 1) * F, b * F : (b + 1) * F], s_high, s_low)

    z0_local = total_faces(PRE0, z0_local)
    wide, _ = gather_finish(0, False)
    z0 = inner_faces([a + b for a, b in zip(z0_local, wide)])

    image = apply_local(z0, s_high, s_low)
    gather_start(1, owned(image), [image[0], image[2]], [(r0, owned(z0)), (z0, image)])
    spread_faces(SCH0, image)
    q0_faces = total_faces(SCH0, image)
    w0_local = apply_local(q0_faces, l_high, l_low)
    spread_faces(PRE1, w0_local)
    gather_forward(1, True)
    w0_local = total_faces(PRE1, w0_local)
    wide, column = gather_finish(1, False)
    rz0, dq0 = column(0), column(1)
    step0 = rz0 / dq0
    w0 = [a + b for a, b in zip(w0_local, wide)]
    z1 = inner_faces([a - step0 * b for a, b in zip(z0, w0)])

    image = apply_local(z1, s_high, s_low)
    q0, z0_own, z1_own = owned(q0_faces), owned(z0), owned(z1)
    r1 = [a - step0 * b for a, b in zip(r0, q0)]
    gather_start(2, owned(image), [image[0], image[2]], [(r1, z1_own), (z1, image), (z0, image), (z1_own, q0)])
    spread_faces(SCH1, image)
    t1_faces = total_faces(SCH1, image)
    w1_local = apply_local(t1_faces, l_high, l_low)
    spread_faces(PRE2, w1_local, True)
    gather_forward(2, True)
    w1_local = total_faces(PRE2, w1_local, True)
    wide, column = gather_finish(2, True)
    w1 = [a + b for a, b in zip(w1_local, wide)]

    t1, w0 = owned(t1_faces), owned(w0)
    rz1 = column(0)
    ratio = rz1 / rz0
    step1 = rz1 / (column(1) + ratio * (column(2) + column(3)) + ratio * ratio * dq0)
    for f in range(2):
        place = slice(f * FP, (f + 1) * FP)
        direction = z1_own[f] + ratio * z0_own[f]
        out_ref[0, :, place] = step0 * z0_own[f] + step1 * direction
        out_ref[1, :, place] = r1[f] - step1 * (t1[f] + ratio * q0[f])
        out_ref[2, :, place] = z1_own[f] - step1 * (w1[f] + ratio * w0[f])

    for copy in started:
        copy.wait_send()

    @pl.when(z == 0)
    def _():
        for phase in range(1, 3):
            for s in range(LZ):
                head_copy(phase, s).wait_send()


def unpad(packed_ref, *out_refs):
    for k, out_ref in enumerate(out_refs):
        out_ref[0, 0, :, :F] = packed_ref[k, :, :F]
        out_ref[0, 0, :, F:] = packed_ref[k, :, FP : FP + F]


def shards(applied_loads, bound_block, coupling, interior_inverse, local_inverse, coarse_inverse):
    dma = pltpu.SemaphoreType.DMA
    packed = pl.pallas_call(
        kernel,
        out_shape=jax.ShapeDtypeStruct((3, K, 2 * FP), f32),
        in_specs=[pl.BlockSpec(memory_space=pltpu.HBM)] * 6,
        out_specs=pl.BlockSpec(memory_space=pltpu.VMEM),
        scratch_shapes=[
            pltpu.VMEM((K, 2 * F), f32),
            pltpu.VMEM((NF, NF), f32),
            pltpu.VMEM((NF, NI), f32),
            pltpu.VMEM((NI, NI), f32),
            pltpu.VMEM((NF, NF), f32),
            pltpu.VMEM((32, NC), f32),
            dma((6,)),
            pltpu.VMEM((NP, NP), bf16),
            pltpu.VMEM((NP, NP), bf16),
            pltpu.VMEM((NP, NP), bf16),
            pltpu.VMEM((NP, NP), bf16),
            pltpu.VMEM((NF, NI), bf16),
            pltpu.VMEM((NF, NI), bf16),
            pltpu.VMEM((NI, COLS), bf16),
            pltpu.VMEM((NI, COLS), bf16),
            pltpu.VMEM((NF, NI), bf16),
            pltpu.VMEM((NF, NI), bf16),
            pltpu.VMEM((NF, NF), f32),
            pltpu.VMEM((2, 32, NC // 2), f32),
            pltpu.VMEM((32, NC // 2), f32),
            pltpu.VMEM((LX * LY, 128, 256), bf16),
            pltpu.VMEM((2 * FP, FP), bf16),
            pltpu.VMEM((FP, 3 * FP), bf16),
            pltpu.VMEM((3, LZ, 8, FP), f32),
            pltpu.VMEM((3, 4, FP), f32),
            pltpu.VMEM((3, LZ, 4, FP), f32),
            pltpu.VMEM((3, 8, FP), f32),
            pltpu.VMEM((3, LX * LY, 40, FP), f32),
            pltpu.VMEM((3, 24, FP), f32),
            pltpu.VMEM((3, 5, 24, FP), f32),
            pltpu.VMEM((SLOTS, K, FP), f32),
            pltpu.VMEM((SLOTS, K, FP), f32),
            dma((3, LZ)),
            dma((3, LZ)),
            dma((3, LZ)),
            dma((3, LZ)),
            dma((3, LZ)),
            dma((3,)),
            dma((3, LX * LY)),
            dma((3, LX * LY)),
            dma,
            dma,
            dma((3, 5)),
            dma((3, 5)),
            dma((SLOTS,)),
            dma((SLOTS,)),
        ],
        compiler_params=pltpu.CompilerParams(
            collective_id=0, has_side_effects=True, vmem_limit_bytes=60 * 1024 * 1024
        ),
    )(applied_loads, bound_block, coupling, interior_inverse, local_inverse, coarse_inverse)
    out = jax.ShapeDtypeStruct((1, 1, K, 2 * F), f32)
    return pl.pallas_call(unpad, out_shape=(out, out, out))(packed)


def solution(mesh):
    blocks = P("sx", "sy", None, None)
    return jax.shard_map(
        shards,
        mesh=mesh,
        in_specs=(blocks, blocks, blocks, blocks, blocks, P(("sx", "sy"), None)),
        out_specs=(blocks, blocks, blocks),
        check_vma=False,
    )
```

```python
import jax
import jax.numpy as jnp
from jax import lax
from jax.experimental import pallas as pl
from jax.experimental.pallas import tpu as pltpu
from jax.sharding import PartitionSpec as P

MESH = pl.DeviceIdType.MESH
F = 96
FP = 128
FACES = 4
K = 16
NF = FACES * F
NP = FACES * FP
NI = 1152
NC = 8192
LX, LY, LZ = 4, 4, 8
COLS = 256
LINE_ORDER = sorted(range(LZ), key=lambda s: min(s, LZ - s))
PLANE_ORDER = sorted(range(LX * LY), key=lambda s: min(s // LX, LY - s // LX) + min(s % LX, LX - s % LX))
f32, bf16 = jnp.float32, jnp.bfloat16

LOADS_W, LOADS_N = 0, 1
PRE0, PRE1, PRE2 = 2, 6, 10
SCH0, SCH1 = 12, 16
SLOTS = 20


def split(value):
    high = value.astype(bf16)
    low = (value - high.astype(f32)).astype(bf16)
    return high, low


def dot(left, right):
    return jnp.dot(left, right, preferred_element_type=f32)


def dot_t(left, right):
    return lax.dot_general(left, right, (((1,), (1,)), ((), ())), preferred_element_type=f32)


def transpose_groups(tiles, lane_group):
    a, b, c, d = tiles
    near = lane_group < 2
    a, c = jnp.where(near, a, pltpu.roll(c, 64, 1)), jnp.where(near, pltpu.roll(a, 64, 1), c)
    b, d = jnp.where(near, b, pltpu.roll(d, 64, 1)), jnp.where(near, pltpu.roll(b, 64, 1), d)
    even = lane_group % 2 == 0
    a, b = jnp.where(even, a, pltpu.roll(b, 32, 1)), jnp.where(even, pltpu.roll(a, 96, 1), b)
    c, d = jnp.where(even, c, pltpu.roll(d, 32, 1)), jnp.where(even, pltpu.roll(c, 96, 1), d)
    return a, b, c, d


def pad_split(get_block, high_ref, low_ref):
    high_ref[...] = jnp.zeros_like(high_ref)
    low_ref[...] = jnp.zeros_like(low_ref)
    for a in range(FACES):
        for b in range(FACES):
            high, low = split(get_block(a, b))
            high_ref[a * FP : a * FP + F, b * FP : b * FP + F] = high
            low_ref[a * FP : a * FP + F, b * FP : b * FP + F] = low


def apply_local(faces, high_ref, low_ref):
    high, low = split(jnp.concatenate(faces, axis=1))
    both = dot(jnp.concatenate([high, low], axis=0), high_ref[...])
    result = both[:K] + both[K:] + dot(high, low_ref[...])
    return [result[:, f * FP : (f + 1) * FP] for f in range(FACES)]


def kernel(
    loads_ref, bound_ref, coupling_ref, interior_ref, local_ref, coarse_ref,
    out_ref,
    loads_v, bound_v, coupling_v, interior_v, local_v, coarse_v, load_sem,
    l_high, l_low, s_high, s_low, c_parts, t_parts, schur_v,
    permuted, partner_rows, coarse_w, restrict_v, spread_v,
    line_v, west_out, west_in, head_in, plane_v, part_out, part_in, halo_out, halo_in,
    line_send, line_recv, west_send, west_recv, head_send, head_recv, plane_send, plane_recv,
    swap_send, swap_recv, part_send, part_recv, halo_send, halo_recv,
):
    i = lax.axis_index("sx")
    j = lax.axis_index("sy")
    y, z = lax.div(i, LZ), lax.rem(i, LZ)
    x, core = lax.div(j, 2), lax.rem(j, 2)
    block = y * LX + x
    east = {"sx": i, "sy": lax.rem(j + 1, 2 * LX)}
    west = {"sx": i, "sy": lax.rem(j + 2 * LX - 1, 2 * LX)}
    south = {"sx": lax.rem(i + 1, LY * LZ), "sy": j}
    north = {"sx": lax.rem(i + LY * LZ - 1, LY * LZ), "sy": j}
    partner = {"sx": i, "sy": x * 2 + (1 - core)}
    line = [{"sx": y * LZ + lax.rem(z + s, LZ), "sy": j} for s in range(LZ)]
    west_line = [{"sx": device["sx"], "sy": west["sy"]} for device in line]
    east_line = [{"sx": device["sx"], "sy": east["sy"]} for device in line]
    north_line = [{"sx": lax.rem(y + LY - 1, LY) * LZ + s, "sy": j} for s in range(LZ)]
    south_head = {"sx": lax.rem(y + 1, LY) * LZ, "sy": j}
    plane = [
        {"sx": lax.rem(y + s // LX, LY) * LZ + z, "sy": lax.rem(x + s % LX, LX) * 2 + core} for s in range(LX * LY)
    ]
    south_pair = [south, {"sx": south["sx"], "sy": partner["sy"]}]
    east_pair = [{"sx": i, "sy": lax.rem(x + 1, LX) * 2 + core}, {"sx": i, "sy": lax.rem(x + 1, LX) * 2 + 1 - core}]
    north_other = {"sx": north["sx"], "sy": partner["sy"]}
    west_other = {"sx": i, "sy": lax.rem(x + LX - 1, LX) * 2 + 1 - core}

    fetches = [
        pltpu.make_async_copy(source, target, load_sem.at[k])
        for k, (source, target) in enumerate(
            [
                (loads_ref.at[0, 0], loads_v),
                (coarse_ref, coarse_v),
                (coupling_ref.at[0, 0], coupling_v),
                (interior_ref.at[0, 0], interior_v),
                (local_ref.at[0, 0], local_v),
                (bound_ref.at[0, 0], bound_v),
            ]
        )
    ]
    fetches[0].start()

    barrier = pltpu.get_barrier_semaphore()
    greeted = [device for s in LINE_ORDER[:0:-1] for device in (east_line[s], line[s])]
    greeted += [plane[s] for s in PLANE_ORDER[:0:-1]]
    greeted += [south_head, north_other, west_other, north, south, east_line[0], east, west, partner]
    for device in greeted:
        pl.semaphore_signal(barrier, 1, device_id=device, device_id_type=MESH)

    for fetch in fetches[1:]:
        fetch.start()

    has_west, has_east = j > 0, j < 2 * LX - 1
    has_north, has_south = i > 0, i < LY * LZ - 1

    def halo_copy(slot, device):
        return pltpu.make_async_remote_copy(
            halo_out.at[slot], halo_in.at[slot], halo_send.at[slot], halo_recv.at[slot], device_id=device, device_id_type=MESH
        )

    def halo_start(slot, device, value):
        halo_out[slot] = value
        copy = halo_copy(slot, device)
        copy.start()
        started.append(copy)

    def halo_wait(slot, device, present):
        halo_copy(slot, device).wait_recv()
        return jnp.where(present, halo_in[slot], 0.0)

    started = []

    lane_row = lax.broadcasted_iota(jnp.int32, (1, FP), 1)
    lane_group = lane_row // 32
    south_lanes = lane_row % 32 >= 16
    case = lax.broadcasted_iota(jnp.int32, (K, FP), 0)
    lane = lax.broadcasted_iota(jnp.int32, (K, FP), 1)
    value_lane = lax.broadcasted_iota(jnp.int32, (2 * FP, FP), 0)
    coarse_lane = lax.broadcasted_iota(jnp.int32, (2 * FP, FP), 1) % 32
    in_face = value_lane % FP
    run_of = (value_lane // FP) * 16 + in_face // 6
    restrict_v[...] = ((run_of == coarse_lane) & (in_face < F)).astype(f32).astype(bf16)
    coarse_at = lax.broadcasted_iota(jnp.int32, (FP, 3 * FP), 0)
    value_at = lax.broadcasted_iota(jnp.int32, (FP, 3 * FP), 1)
    value_in = value_at % FP
    face_at = value_at // FP
    first = jnp.where(face_at == 2, (1 - core) * 32, core * 32 + face_at * 16)
    spread_v[...] = ((first + value_in // 6 == coarse_at) & (value_in < F)).astype(f32).astype(bf16)

    def line_copy(phase, s):
        return pltpu.make_async_remote_copy(
            line_v.at[phase, z], line_v.at[phase, z], line_send.at[phase, s], line_recv.at[phase, s],
            device_id=line[s], device_id_type=MESH,
        )

    def west_copy(phase, s):
        return pltpu.make_async_remote_copy(
            west_out.at[phase], west_in.at[phase, z], west_send.at[phase, s], west_recv.at[phase, s],
            device_id=west_line[s], device_id_type=MESH,
        )

    def head_copy(phase, s):
        return pltpu.make_async_remote_copy(
            line_v.at[phase, z], head_in.at[phase], head_send.at[phase, s], head_recv.at[phase],
            device_id=north_line[s], device_id_type=MESH,
        )

    def plane_copy(phase, s):
        rows = pl.ds(0, 40 if phase else 32)
        return pltpu.make_async_remote_copy(
            plane_v.at[phase, block, rows], plane_v.at[phase, block, rows], plane_send.at[phase, s], plane_recv.at[phase, s],
            device_id=plane[s], device_id_type=MESH,
        )

    def part_copy(phase, k, slot, device):
        rows = pl.ds(0, 16 if k == 4 else 8)
        return pltpu.make_async_remote_copy(
            part_out.at[phase, rows], part_in.at[phase, slot, rows], part_send.at[phase, k], part_recv.at[phase, slot],
            device_id=device, device_id_type=MESH,
        )

    def go(copy):
        copy.start()
        started.append(copy)

    def pack(sums):
        packed = sums[:4]
        for q in range(1, 4):
            packed = jnp.where(lane_group == q, sums[4 * q : 4 * q + 4], packed)
        return packed

    def gather_start(phase, own, shared, dots):
        values = [jnp.concatenate(own, axis=1)] + ([jnp.concatenate(shared, axis=1)] if shared else [])
        high, low = split(jnp.concatenate(values, axis=0))
        rows = len(values) * K
        sums = dot(jnp.concatenate([high, low], axis=0), restrict_v[...])
        sums = sums[:rows] + sums[rows:]
        line_v[phase, z, :4] = pack(sums[:K])
        if not shared:
            line_v[phase, z, 4:] = jnp.zeros((4, FP), f32)
        else:
            others = pack(sums[K:])
            west_out[phase] = others
            for s in LINE_ORDER[::-1]:
                go(west_copy(phase, s))
            placed = jnp.zeros((K, FP), f32)
            for d, (left, right) in enumerate(dots):
                product = left[0] * right[0]
                for f in range(1, len(left)):
                    product += left[f] * right[f]
                placed = jnp.where(lane == d * 32 + case, jnp.sum(product, axis=1, keepdims=True), placed)
            row = jnp.sum(placed, axis=0, keepdims=True)
            line_v[phase, z, 4:] = jnp.where(south_lanes, others, row)

            @pl.when(z == 0)
            def _():
                for s in range(LZ):
                    head_copy(phase, s).start()

        for s in LINE_ORDER[:0:-1]:
            go(line_copy(phase, s))

    def gather_forward(phase, shared):
        for s in range(1, LZ):
            line_copy(phase, s).wait_recv()
        if shared:
            for s in range(LZ):
                west_copy(phase, s).wait_recv()
            head_copy(phase, 0).wait_recv()
        tiles = []
        for s in range(LZ):
            tile = line_v[phase, s, :4]
            if shared:
                if s + 1 < LZ:
                    below = line_v[phase, s + 1, 4:]
                else:
                    below = jnp.where(y < LY - 1, head_in[phase, 4:], 0.0)
                right = jnp.where(has_east, west_in[phase, s], 0.0)
                tile = tile + jnp.where(south_lanes, below, right)
            tiles.append(tile)
        pairs = [jnp.concatenate([tiles[d], tiles[4 + d]], axis=0) for d in range(4)]
        for q, mixed in enumerate(transpose_groups(pairs, lane_group)):
            plane_v[phase, block, 4 * q : 4 * q + 4] = mixed[:4]
            plane_v[phase, block, K + 4 * q : K + 4 * q + 4] = mixed[4:]
        if shared:
            total = line_v[phase, 0]
            for s in range(1, LZ):
                total = total + line_v[phase, s]
            plane_v[phase, block, 2 * K :] = total
        for s in PLANE_ORDER[:0:-1]:
            go(plane_copy(phase, s))

    def gather_finish(phase, last, scalars=None):
        total = jnp.zeros((2 * K, FP), f32)
        sums = jnp.zeros((8, FP), f32)
        for group in (PLANE_ORDER[:11], PLANE_ORDER[11:]):
            for s in group:
                if s:
                    plane_copy(phase, s).wait_recv()
            for s in group:
                b = lax.rem(y + LY - s // LX, LY) * LX + lax.rem(x + LX - s % LX, LX)
                value = jnp.concatenate([plane_v[phase, b, :K], plane_v[phase, b, K : 2 * K]], axis=1)
                high, low = split(value)
                total += dot_t(jnp.concatenate([high, low], axis=0), coarse_w[b])
                if phase:
                    sums += plane_v[phase, b, 2 * K :]
        part = total[:K] + total[K:]
        part = part + pltpu.roll(part, 64, 1)
        part = jnp.where(lane_row < 64, part[:8], part[8:])
        part_out[phase, :8] = part
        part_out[phase, 8:] = sums
        if not last:
            for k in range(2):
                go(part_copy(phase, k, 1 + core, south_pair[k]))
                go(part_copy(phase, 2 + k, 3 + core, east_pair[k]))
        go(part_copy(phase, 4, 0, partner))
        part_copy(phase, 4, 0, partner).wait_recv()
        own = part + part_in[phase, 0, :8]
        sums = sums + part_in[phase, 0, 8:]

        def column(d):
            return jnp.sum(jnp.where(lane == d * 32 + case, sums[4:5], 0.0), axis=1, keepdims=True)

        values = scalars(column) if scalars else None
        groups = [own]
        if not last:
            for slot in range(1, 5):
                part_copy(phase, 0, slot, partner).wait_recv()
            groups.append(part_in[phase, 1, :8] + part_in[phase, 2, :8])
            groups.append(jnp.where(core == 0, part_in[phase, 3, :8] + part_in[phase, 4, :8], own))
        high, low = split(jnp.concatenate([half for t in groups for half in (t, pltpu.roll(t, 64, 1))], axis=0))
        rows = len(groups) * K
        wide = dot(jnp.concatenate([high, low], axis=0), spread_v[...])
        wide = wide[:rows] + wide[rows:]
        faces = [wide[:K, :FP], wide[:K, FP : 2 * FP]]
        if not last:
            faces = [wide[2 * K :, 2 * FP :], faces[0], wide[K : 2 * K, FP : 2 * FP], faces[1]]
        return faces, values

    def spread_faces(slot, result, last=False):
        halo_start(slot, west, result[0])
        halo_start(slot + 1, north, result[2])
        if not last:
            halo_start(slot + 2, east, result[1])
            halo_start(slot + 3, south, result[3])

    def total_faces(slot, result, last=False):
        east_total = result[1] + halo_wait(slot, west, has_east)
        south_total = result[3] + halo_wait(slot + 1, north, has_south)
        if last:
            return [east_total, south_total]
        west_total = result[0] + halo_wait(slot + 2, east, has_west)
        north_total = result[2] + halo_wait(slot + 3, south, has_north)
        return inner_faces([west_total, east_total, north_total, south_total])

    def inner_faces(faces):
        return [jnp.where(has_west, faces[0], 0.0), faces[1], jnp.where(has_north, faces[2], 0.0), faces[3]]

    def owned(faces):
        return [faces[1], faces[3]]

    fetches[0].wait()
    padding = jnp.zeros((K, FP - F), f32)
    r0 = [
        jnp.concatenate([loads_v[:, :F], padding], axis=1),
        jnp.concatenate([loads_v[:, F : 2 * F], padding], axis=1),
    ]

    pl.semaphore_wait(barrier, len(greeted) - 1 + LZ * lax.div(LZ - 1 - z, LZ - 1))

    gather_start(0, r0, None, None)
    halo_start(LOADS_W, east, r0[0])
    halo_start(LOADS_N, south, r0[1])

    fetches[1].wait()

    def permute(step, _):
        y_at, rest = lax.div(step, 4), lax.rem(step, 4)
        half, j_half = lax.div(rest, 2), lax.rem(rest, 2)
        tiles = []
        for d in range(4):
            at = ((y_at * LZ + half * 4 + d) * 2 + j_half) * FP
            tiles.append(coarse_v[:, pl.ds(pl.multiple_of(at, FP), FP)])
        for q, mixed in enumerate(transpose_groups(tiles, lane_group)):
            at = (y_at * LX + j_half * 2 + q // 2) * 256 + half * FP
            permuted[q % 2, :, pl.ds(pl.multiple_of(at, FP), FP)] = mixed
        return 0

    lax.fori_loop(0, 16, permute, 0)
    swap = pltpu.make_async_remote_copy(
        permuted.at[1 - core], partner_rows, swap_send, swap_recv, device_id=partner, device_id_type=MESH
    )
    go(swap)

    def interior_columns(columns):
        i_high, i_low = split(interior_v[:, columns])
        both = dot(c_parts[...], i_high)
        total = both[:NF] + both[NF:] + dot(c_parts[:NF], i_low)
        t_parts[:NF, columns], t_parts[NF:, columns] = split(total)

    def times_interior(step, _):
        interior_columns(pl.ds(pl.multiple_of(step * COLS, FP), COLS))
        return 0

    fetches[2].wait()
    c_parts[:NF], c_parts[NF:] = split(coupling_v[...])
    fetches[3].wait()
    lax.fori_loop(0, 2, times_interior, 0)

    fetches[4].wait()
    pad_split(lambda a, b: local_v[a * F : (a + 1) * F, b * F : (b + 1) * F], l_high, l_low)
    from_west = halo_wait(LOADS_W, east, has_west)
    from_north = halo_wait(LOADS_N, south, has_north)
    z0_local = apply_local([from_west, r0[0], from_north, r0[1]], l_high, l_low)
    spread_faces(PRE0, z0_local)

    gather_forward(0, False)

    def place_rows(value, at):
        high, low = split(value)
        for b in range(LX * LY):
            coarse_w[b, pl.ds(pl.multiple_of(at, 32), 32)] = high[:, b * 256 : (b + 1) * 256]
            coarse_w[b, pl.ds(pl.multiple_of(64 + at, 32), 32)] = low[:, b * 256 : (b + 1) * 256]

    place_rows(permuted[core], core * 32)
    swap.wait_recv()
    place_rows(partner_rows[...], (1 - core) * 32)
    lax.fori_loop(2, NI // COLS, times_interior, 0)
    interior_columns(slice(NI // COLS * COLS, NI))
    back = dot_t(t_parts[...], c_parts[:NF])
    back = back[:NF] + back[NF:] + dot_t(t_parts[:NF], c_parts[NF:])
    fetches[5].wait()
    schur_v[...] = bound_v[...] - back
    pad_split(lambda a, b: schur_v[a * F : (a + 1) * F, b * F : (b + 1) * F], s_high, s_low)

    z0_local = total_faces(PRE0, z0_local)
    wide, _ = gather_finish(0, False)
    z0 = inner_faces([a + b for a, b in zip(z0_local, wide)])

    image = apply_local(z0, s_high, s_low)
    gather_start(1, owned(image), [image[0], image[2]], [(r0, owned(z0)), (z0, image)])
    spread_faces(SCH0, image)
    q0_faces = total_faces(SCH0, image)
    w0_local = apply_local(q0_faces, l_high, l_low)
    spread_faces(PRE1, w0_local)
    gather_forward(1, True)
    w0_local = total_faces(PRE1, w0_local)

    def first_step(column):
        rz0, dq0 = column(0), column(1)
        return rz0, dq0, rz0 / dq0

    wide, (rz0, dq0, step0) = gather_finish(1, False, first_step)
    w0 = [a + b for a, b in zip(w0_local, wide)]
    z1 = inner_faces([a - step0 * b for a, b in zip(z0, w0)])

    image = apply_local(z1, s_high, s_low)
    q0, z0_own, z1_own = owned(q0_faces), owned(z0), owned(z1)
    r1 = [a - step0 * b for a, b in zip(r0, q0)]
    gather_start(2, owned(image), [image[0], image[2]], [(r1, z1_own), (z1, image), (z0, image), (z1_own, q0)])
    spread_faces(SCH1, image)
    t1_faces = total_faces(SCH1, image)
    w1_local = apply_local(t1_faces, l_high, l_low)
    spread_faces(PRE2, w1_local, True)
    gather_forward(2, True)
    w1_local = total_faces(PRE2, w1_local, True)

    def second_step(column):
        rz1 = column(0)
        ratio = rz1 / rz0
        return ratio, rz1 / (column(1) + ratio * (column(2) + column(3)) + ratio * ratio * dq0)

    wide, (ratio, step1) = gather_finish(2, True, second_step)
    w1 = [a + b for a, b in zip(w1_local, wide)]

    t1, w0 = owned(t1_faces), owned(w0)
    for f in range(2):
        place = slice(f * FP, (f + 1) * FP)
        direction = z1_own[f] + ratio * z0_own[f]
        out_ref[0, :, place] = step0 * z0_own[f] + step1 * direction
        out_ref[1, :, place] = r1[f] - step1 * (t1[f] + ratio * q0[f])
        out_ref[2, :, place] = z1_own[f] - step1 * (w1[f] + ratio * w0[f])

    for copy in started:
        copy.wait_send()

    @pl.when(z == 0)
    def _():
        for phase in range(1, 3):
            for s in range(LZ):
                head_copy(phase, s).wait_send()


def unpad(packed_ref, *out_refs):
    for k, out_ref in enumerate(out_refs):
        out_ref[0, 0, :, :F] = packed_ref[k, :, :F]
        out_ref[0, 0, :, F:] = packed_ref[k, :, FP : FP + F]


def shards(applied_loads, bound_block, coupling, interior_inverse, local_inverse, coarse_inverse):
    dma = pltpu.SemaphoreType.DMA
    packed = pl.pallas_call(
        kernel,
        out_shape=jax.ShapeDtypeStruct((3, K, 2 * FP), f32),
        in_specs=[pl.BlockSpec(memory_space=pltpu.HBM)] * 6,
        out_specs=pl.BlockSpec(memory_space=pltpu.VMEM),
        scratch_shapes=[
            pltpu.VMEM((K, 2 * F), f32),
            pltpu.VMEM((NF, NF), f32),
            pltpu.VMEM((NF, NI), f32),
            pltpu.VMEM((NI, NI), f32),
            pltpu.VMEM((NF, NF), f32),
            pltpu.VMEM((32, NC), f32),
            dma((6,)),
            pltpu.VMEM((NP, NP), bf16),
            pltpu.VMEM((NP, NP), bf16),
            pltpu.VMEM((NP, NP), bf16),
            pltpu.VMEM((NP, NP), bf16),
            pltpu.VMEM((2 * NF, NI), bf16),
            pltpu.VMEM((2 * NF, NI), bf16),
            pltpu.VMEM((NF, NF), f32),
            pltpu.VMEM((2, 32, NC // 2), f32),
            pltpu.VMEM((32, NC // 2), f32),
            pltpu.VMEM((LX * LY, 128, 256), bf16),
            pltpu.VMEM((2 * FP, FP), bf16),
            pltpu.VMEM((FP, 3 * FP), bf16),
            pltpu.VMEM((3, LZ, 8, FP), f32),
            pltpu.VMEM((3, 4, FP), f32),
            pltpu.VMEM((3, LZ, 4, FP), f32),
            pltpu.VMEM((3, 8, FP), f32),
            pltpu.VMEM((3, LX * LY, 40, FP), f32),
            pltpu.VMEM((3, 16, FP), f32),
            pltpu.VMEM((3, 5, 16, FP), f32),
            pltpu.VMEM((SLOTS, K, FP), f32),
            pltpu.VMEM((SLOTS, K, FP), f32),
            dma((3, LZ)),
            dma((3, LZ)),
            dma((3, LZ)),
            dma((3, LZ)),
            dma((3, LZ)),
            dma((3,)),
            dma((3, LX * LY)),
            dma((3, LX * LY)),
            dma,
            dma,
            dma((3, 5)),
            dma((3, 5)),
            dma((SLOTS,)),
            dma((SLOTS,)),
        ],
        compiler_params=pltpu.CompilerParams(
            collective_id=0, has_side_effects=True, vmem_limit_bytes=60 * 1024 * 1024
        ),
    )(applied_loads, bound_block, coupling, interior_inverse, local_inverse, coarse_inverse)
    out = jax.ShapeDtypeStruct((1, 1, K, 2 * F), f32)
    return pl.pallas_call(unpad, out_shape=(out, out, out))(packed)


def solution(mesh):
    blocks = P("sx", "sy", None, None)
    return jax.shard_map(
        shards,
        mesh=mesh,
        in_specs=(blocks, blocks, blocks, blocks, blocks, P(("sx", "sy"), None)),
        out_specs=(blocks, blocks, blocks),
        check_vma=False,
    )
```

```python
import jax
import jax.numpy as jnp
from jax import lax
from jax.experimental import pallas as pl
from jax.experimental.pallas import tpu as pltpu
from jax.sharding import PartitionSpec as P

MESH = pl.DeviceIdType.MESH
F = 96
FP = 128
FACES = 4
K = 16
NF = FACES * F
NP = FACES * FP
NI = 1152
NC = 8192
LX, LY, LZ = 4, 4, 8
COLS = 256
LINE_ORDER = sorted(range(LZ), key=lambda s: min(s, LZ - s))
PLANE_ORDER = sorted(range(LX * LY), key=lambda s: min(s // LX, LY - s // LX) + min(s % LX, LX - s % LX))
f32, bf16 = jnp.float32, jnp.bfloat16

LOADS_W, LOADS_N = 0, 1
PRE0, PRE1, PRE2 = 2, 6, 10
SCH0, SCH1 = 12, 16
SLOTS = 20


def split(value):
    high = value.astype(bf16)
    low = (value - high.astype(f32)).astype(bf16)
    return high, low


def dot(left, right):
    return jnp.dot(left, right, preferred_element_type=f32)


def dot_t(left, right):
    return lax.dot_general(left, right, (((1,), (1,)), ((), ())), preferred_element_type=f32)


def transpose_groups(tiles, lane_group):
    a, b, c, d = tiles
    near = lane_group < 2
    a, c = jnp.where(near, a, pltpu.roll(c, 64, 1)), jnp.where(near, pltpu.roll(a, 64, 1), c)
    b, d = jnp.where(near, b, pltpu.roll(d, 64, 1)), jnp.where(near, pltpu.roll(b, 64, 1), d)
    even = lane_group % 2 == 0
    a, b = jnp.where(even, a, pltpu.roll(b, 32, 1)), jnp.where(even, pltpu.roll(a, 96, 1), b)
    c, d = jnp.where(even, c, pltpu.roll(d, 32, 1)), jnp.where(even, pltpu.roll(c, 96, 1), d)
    return a, b, c, d


def pad_split(get_block, high_ref, low_ref):
    high_ref[...] = jnp.zeros_like(high_ref)
    low_ref[...] = jnp.zeros_like(low_ref)
    for a in range(FACES):
        for b in range(FACES):
            high, low = split(get_block(a, b))
            high_ref[a * FP : a * FP + F, b * FP : b * FP + F] = high
            low_ref[a * FP : a * FP + F, b * FP : b * FP + F] = low


def apply_local(faces, high_ref, low_ref):
    high, low = split(jnp.concatenate(faces, axis=1))
    both = dot(jnp.concatenate([high, low], axis=0), high_ref[...])
    result = both[:K] + both[K:] + dot(high, low_ref[...])
    return [result[:, f * FP : (f + 1) * FP] for f in range(FACES)]


def kernel(
    loads_ref, bound_ref, coupling_ref, interior_ref, local_ref, coarse_ref,
    out_ref,
    loads_v, bound_v, coupling_v, interior_v, local_v, coarse_v, load_sem,
    l_high, l_low, s_high, s_low, c_parts, t_parts, schur_v,
    permuted, partner_rows, coarse_w, restrict_v, spread_v,
    line_v, west_out, west_in, head_in, plane_v, part_out, part_in, halo_out, halo_in,
    line_send, line_recv, west_send, west_recv, head_send, head_recv, plane_send, plane_recv,
    swap_send, swap_recv, part_send, part_recv, halo_send, halo_recv,
):
    i = lax.axis_index("sx")
    j = lax.axis_index("sy")
    y, z = lax.div(i, LZ), lax.rem(i, LZ)
    x, core = lax.div(j, 2), lax.rem(j, 2)
    block = y * LX + x
    east = {"sx": i, "sy": lax.rem(j + 1, 2 * LX)}
    west = {"sx": i, "sy": lax.rem(j + 2 * LX - 1, 2 * LX)}
    south = {"sx": lax.rem(i + 1, LY * LZ), "sy": j}
    north = {"sx": lax.rem(i + LY * LZ - 1, LY * LZ), "sy": j}
    partner = {"sx": i, "sy": x * 2 + (1 - core)}
    line = [{"sx": y * LZ + lax.rem(z + s, LZ), "sy": j} for s in range(LZ)]
    west_line = [{"sx": device["sx"], "sy": west["sy"]} for device in line]
    east_line = [{"sx": device["sx"], "sy": east["sy"]} for device in line]
    north_line = [{"sx": lax.rem(y + LY - 1, LY) * LZ + s, "sy": j} for s in range(LZ)]
    south_head = {"sx": lax.rem(y + 1, LY) * LZ, "sy": j}
    plane = [
        {"sx": lax.rem(y + s // LX, LY) * LZ + z, "sy": lax.rem(x + s % LX, LX) * 2 + core} for s in range(LX * LY)
    ]
    south_pair = [south, {"sx": south["sx"], "sy": partner["sy"]}]
    east_pair = [{"sx": i, "sy": lax.rem(x + 1, LX) * 2 + core}, {"sx": i, "sy": lax.rem(x + 1, LX) * 2 + 1 - core}]
    north_other = {"sx": north["sx"], "sy": partner["sy"]}
    west_other = {"sx": i, "sy": lax.rem(x + LX - 1, LX) * 2 + 1 - core}

    fetches = [
        pltpu.make_async_copy(source, target, load_sem.at[k])
        for k, (source, target) in enumerate(
            [
                (loads_ref.at[0, 0], loads_v),
                (coarse_ref, coarse_v),
                (coupling_ref.at[0, 0], coupling_v),
                (interior_ref.at[0, 0], interior_v),
                (local_ref.at[0, 0], local_v),
                (bound_ref.at[0, 0], bound_v),
            ]
        )
    ]
    fetches[0].start()

    barrier = pltpu.get_barrier_semaphore()
    greeted = [device for s in LINE_ORDER[:0:-1] for device in (east_line[s], line[s])]
    greeted += [plane[s] for s in PLANE_ORDER[:0:-1]]
    greeted += [south_head, north_other, west_other, north, south, east_line[0], east, west, partner]
    for device in greeted:
        pl.semaphore_signal(barrier, 1, device_id=device, device_id_type=MESH)

    for fetch in fetches[1:]:
        fetch.start()

    has_west, has_east = j > 0, j < 2 * LX - 1
    has_north, has_south = i > 0, i < LY * LZ - 1

    def halo_copy(slot, device):
        return pltpu.make_async_remote_copy(
            halo_out.at[slot], halo_in.at[slot], halo_send.at[slot], halo_recv.at[slot], device_id=device, device_id_type=MESH
        )

    def halo_start(slot, device, value):
        halo_out[slot] = value
        copy = halo_copy(slot, device)
        copy.start()
        started.append(copy)

    def halo_wait(slot, device, present):
        halo_copy(slot, device).wait_recv()
        return jnp.where(present, halo_in[slot], 0.0)

    started = []

    lane_row = lax.broadcasted_iota(jnp.int32, (1, FP), 1)
    lane_group = lane_row // 32
    south_lanes = lane_row % 32 >= 16
    case = lax.broadcasted_iota(jnp.int32, (K, FP), 0)
    lane = lax.broadcasted_iota(jnp.int32, (K, FP), 1)
    value_lane = lax.broadcasted_iota(jnp.int32, (2 * FP, FP), 0)
    coarse_lane = lax.broadcasted_iota(jnp.int32, (2 * FP, FP), 1) % 32
    in_face = value_lane % FP
    run_of = (value_lane // FP) * 16 + in_face // 6
    restrict_v[...] = ((run_of == coarse_lane) & (in_face < F)).astype(f32).astype(bf16)
    coarse_at = lax.broadcasted_iota(jnp.int32, (FP, 3 * FP), 0)
    value_at = lax.broadcasted_iota(jnp.int32, (FP, 3 * FP), 1)
    value_in = value_at % FP
    face_at = value_at // FP
    first = jnp.where(face_at == 2, (1 - core) * 32, core * 32 + face_at * 16)
    spread_v[...] = ((first + value_in // 6 == coarse_at) & (value_in < F)).astype(f32).astype(bf16)

    def line_copy(phase, s):
        return pltpu.make_async_remote_copy(
            line_v.at[phase, z], line_v.at[phase, z], line_send.at[phase, s], line_recv.at[phase, s],
            device_id=line[s], device_id_type=MESH,
        )

    def west_copy(phase, s):
        return pltpu.make_async_remote_copy(
            west_out.at[phase], west_in.at[phase, z], west_send.at[phase, s], west_recv.at[phase, s],
            device_id=west_line[s], device_id_type=MESH,
        )

    def head_copy(phase, s):
        return pltpu.make_async_remote_copy(
            line_v.at[phase, z], head_in.at[phase], head_send.at[phase, s], head_recv.at[phase],
            device_id=north_line[s], device_id_type=MESH,
        )

    def plane_copy(phase, s):
        rows = pl.ds(0, 40 if phase else 32)
        return pltpu.make_async_remote_copy(
            plane_v.at[phase, block, rows], plane_v.at[phase, block, rows], plane_send.at[phase, s], plane_recv.at[phase, s],
            device_id=plane[s], device_id_type=MESH,
        )

    def part_copy(phase, k, slot, device):
        rows = pl.ds(0, 16 if k == 4 else 8)
        return pltpu.make_async_remote_copy(
            part_out.at[phase, rows], part_in.at[phase, slot, rows], part_send.at[phase, k], part_recv.at[phase, slot],
            device_id=device, device_id_type=MESH,
        )

    def go(copy):
        copy.start()
        started.append(copy)

    def pack(sums):
        packed = sums[:4]
        for q in range(1, 4):
            packed = jnp.where(lane_group == q, sums[4 * q : 4 * q + 4], packed)
        return packed

    def gather_start(phase, own, shared, dots):
        values = [jnp.concatenate(own, axis=1)] + ([jnp.concatenate(shared, axis=1)] if shared else [])
        high, low = split(jnp.concatenate(values, axis=0))
        rows = len(values) * K
        sums = dot(jnp.concatenate([high, low], axis=0), restrict_v[...])
        sums = sums[:rows] + sums[rows:]
        line_v[phase, z, :4] = pack(sums[:K])
        if not shared:
            line_v[phase, z, 4:] = jnp.zeros((4, FP), f32)
        else:
            others = pack(sums[K:])
            west_out[phase] = others
            for s in LINE_ORDER[::-1]:
                go(west_copy(phase, s))
            placed = jnp.zeros((K, FP), f32)
            for d, (left, right) in enumerate(dots):
                product = left[0] * right[0]
                for f in range(1, len(left)):
                    product += left[f] * right[f]
                placed = jnp.where(lane == d * 32 + case, jnp.sum(product, axis=1, keepdims=True), placed)
            row = jnp.sum(placed, axis=0, keepdims=True)
            line_v[phase, z, 4:] = jnp.where(south_lanes, others, row)

            @pl.when(z == 0)
            def _():
                for s in range(LZ):
                    head_copy(phase, s).start()

        for s in LINE_ORDER[:0:-1]:
            go(line_copy(phase, s))

    def gather_forward(phase, shared):
        for s in range(1, LZ):
            line_copy(phase, s).wait_recv()
        if shared:
            for s in range(LZ):
                west_copy(phase, s).wait_recv()
            head_copy(phase, 0).wait_recv()
        tiles = []
        for s in range(LZ):
            tile = line_v[phase, s, :4]
            if shared:
                if s + 1 < LZ:
                    below = line_v[phase, s + 1, 4:]
                else:
                    below = jnp.where(y < LY - 1, head_in[phase, 4:], 0.0)
                right = jnp.where(has_east, west_in[phase, s], 0.0)
                tile = tile + jnp.where(south_lanes, below, right)
            tiles.append(tile)
        pairs = [jnp.concatenate([tiles[d], tiles[4 + d]], axis=0) for d in range(4)]
        for q, mixed in enumerate(transpose_groups(pairs, lane_group)):
            plane_v[phase, block, 4 * q : 4 * q + 4] = mixed[:4]
            plane_v[phase, block, K + 4 * q : K + 4 * q + 4] = mixed[4:]
        if shared:
            total = line_v[phase, 0]
            for s in range(1, LZ):
                total = total + line_v[phase, s]
            plane_v[phase, block, 2 * K :] = total
        for s in PLANE_ORDER[:0:-1]:
            go(plane_copy(phase, s))

    def gather_finish(phase, last, scalars=None):
        total = jnp.zeros((2 * K, FP), f32)
        sums = jnp.zeros((8, FP), f32)
        for group in (PLANE_ORDER[:5], PLANE_ORDER[5:11], PLANE_ORDER[11:]):
            for s in group:
                if s:
                    plane_copy(phase, s).wait_recv()
            for s in group:
                b = lax.rem(y + LY - s // LX, LY) * LX + lax.rem(x + LX - s % LX, LX)
                value = jnp.concatenate([plane_v[phase, b, :K], plane_v[phase, b, K : 2 * K]], axis=1)
                high, low = split(value)
                total += dot_t(jnp.concatenate([high, low], axis=0), coarse_w[b])
                if phase:
                    sums += plane_v[phase, b, 2 * K :]
        part = total[:K] + total[K:]
        part = part + pltpu.roll(part, 64, 1)
        part = jnp.where(lane_row < 64, part[:8], part[8:])
        part_out[phase, :8] = part
        part_out[phase, 8:] = sums
        if not last:
            for k in range(2):
                go(part_copy(phase, k, 1 + core, south_pair[k]))
                go(part_copy(phase, 2 + k, 3 + core, east_pair[k]))
        go(part_copy(phase, 4, 0, partner))
        part_copy(phase, 4, 0, partner).wait_recv()
        own = part + part_in[phase, 0, :8]
        sums = sums + part_in[phase, 0, 8:]

        def column(d):
            return jnp.sum(jnp.where(lane == d * 32 + case, sums[4:5], 0.0), axis=1, keepdims=True)

        values = scalars(column) if scalars else None
        groups = [own]
        if not last:
            for slot in range(1, 5):
                part_copy(phase, 0, slot, partner).wait_recv()
            groups.append(part_in[phase, 1, :8] + part_in[phase, 2, :8])
            groups.append(jnp.where(core == 0, part_in[phase, 3, :8] + part_in[phase, 4, :8], own))
        high, low = split(jnp.concatenate([half for t in groups for half in (t, pltpu.roll(t, 64, 1))], axis=0))
        rows = len(groups) * K
        wide = dot(jnp.concatenate([high, low], axis=0), spread_v[...])
        wide = wide[:rows] + wide[rows:]
        faces = [wide[:K, :FP], wide[:K, FP : 2 * FP]]
        if not last:
            faces = [wide[2 * K :, 2 * FP :], faces[0], wide[K : 2 * K, FP : 2 * FP], faces[1]]
        return faces, values

    def spread_faces(slot, result, last=False):
        halo_start(slot, west, result[0])
        halo_start(slot + 1, north, result[2])
        if not last:
            halo_start(slot + 2, east, result[1])
            halo_start(slot + 3, south, result[3])

    def total_faces(slot, result, last=False):
        east_total = result[1] + halo_wait(slot, west, has_east)
        south_total = result[3] + halo_wait(slot + 1, north, has_south)
        if last:
            return [east_total, south_total]
        west_total = result[0] + halo_wait(slot + 2, east, has_west)
        north_total = result[2] + halo_wait(slot + 3, south, has_north)
        return inner_faces([west_total, east_total, north_total, south_total])

    def inner_faces(faces):
        return [jnp.where(has_west, faces[0], 0.0), faces[1], jnp.where(has_north, faces[2], 0.0), faces[3]]

    def owned(faces):
        return [faces[1], faces[3]]

    fetches[0].wait()
    padding = jnp.zeros((K, FP - F), f32)
    r0 = [
        jnp.concatenate([loads_v[:, :F], padding], axis=1),
        jnp.concatenate([loads_v[:, F : 2 * F], padding], axis=1),
    ]

    fetches[1].wait()

    def permute(step, _):
        y_at, rest = lax.div(step, 4), lax.rem(step, 4)
        half, j_half = lax.div(rest, 2), lax.rem(rest, 2)
        tiles = []
        for d in range(4):
            at = ((y_at * LZ + half * 4 + d) * 2 + j_half) * FP
            tiles.append(coarse_v[:, pl.ds(pl.multiple_of(at, FP), FP)])
        for q, mixed in enumerate(transpose_groups(tiles, lane_group)):
            at = (y_at * LX + j_half * 2 + q // 2) * 256 + half * FP
            permuted[q % 2, :, pl.ds(pl.multiple_of(at, FP), FP)] = mixed
        return 0

    lax.fori_loop(0, 16, permute, 0)
    pl.semaphore_wait(barrier, len(greeted) - 1 + LZ * lax.div(LZ - 1 - z, LZ - 1))

    gather_start(0, r0, None, None)
    halo_start(LOADS_W, east, r0[0])
    halo_start(LOADS_N, south, r0[1])

    swap = pltpu.make_async_remote_copy(
        permuted.at[1 - core], partner_rows, swap_send, swap_recv, device_id=partner, device_id_type=MESH
    )
    go(swap)

    def interior_columns(columns):
        i_high, i_low = split(interior_v[:, columns])
        both = dot(c_parts[...], i_high)
        total = both[:NF] + both[NF:] + dot(c_parts[:NF], i_low)
        t_parts[:NF, columns], t_parts[NF:, columns] = split(total)

    def times_interior(step, _):
        interior_columns(pl.ds(pl.multiple_of(step * COLS, FP), COLS))
        return 0

    fetches[2].wait()
    c_parts[:NF], c_parts[NF:] = split(coupling_v[...])
    fetches[3].wait()
    lax.fori_loop(0, 2, times_interior, 0)

    fetches[4].wait()
    pad_split(lambda a, b: local_v[a * F : (a + 1) * F, b * F : (b + 1) * F], l_high, l_low)
    from_west = halo_wait(LOADS_W, east, has_west)
    from_north = halo_wait(LOADS_N, south, has_north)
    z0_local = apply_local([from_west, r0[0], from_north, r0[1]], l_high, l_low)
    spread_faces(PRE0, z0_local)

    gather_forward(0, False)

    def place_rows(value, at):
        high, low = split(value)
        for b in range(LX * LY):
            coarse_w[b, pl.ds(pl.multiple_of(at, 32), 32)] = high[:, b * 256 : (b + 1) * 256]
            coarse_w[b, pl.ds(pl.multiple_of(64 + at, 32), 32)] = low[:, b * 256 : (b + 1) * 256]

    place_rows(permuted[core], core * 32)
    swap.wait_recv()
    place_rows(partner_rows[...], (1 - core) * 32)
    lax.fori_loop(2, NI // COLS, times_interior, 0)
    interior_columns(slice(NI // COLS * COLS, NI))
    back = dot_t(t_parts[...], c_parts[:NF])
    back = back[:NF] + back[NF:] + dot_t(t_parts[:NF], c_parts[NF:])
    fetches[5].wait()
    schur_v[...] = bound_v[...] - back
    pad_split(lambda a, b: schur_v[a * F : (a + 1) * F, b * F : (b + 1) * F], s_high, s_low)

    z0_local = total_faces(PRE0, z0_local)
    wide, _ = gather_finish(0, False)
    z0 = inner_faces([a + b for a, b in zip(z0_local, wide)])

    image = apply_local(z0, s_high, s_low)
    gather_start(1, owned(image), [image[0], image[2]], [(r0, owned(z0)), (z0, image)])
    spread_faces(SCH0, image)
    q0_faces = total_faces(SCH0, image)
    w0_local = apply_local(q0_faces, l_high, l_low)
    spread_faces(PRE1, w0_local)
    gather_forward(1, True)
    w0_local = total_faces(PRE1, w0_local)

    def first_step(column):
        rz0, dq0 = column(0), column(1)
        return rz0, dq0, rz0 / dq0

    wide, (rz0, dq0, step0) = gather_finish(1, False, first_step)
    w0 = [a + b for a, b in zip(w0_local, wide)]
    z1 = inner_faces([a - step0 * b for a, b in zip(z0, w0)])

    image = apply_local(z1, s_high, s_low)
    q0, z0_own, z1_own = owned(q0_faces), owned(z0), owned(z1)
    r1 = [a - step0 * b for a, b in zip(r0, q0)]
    gather_start(2, owned(image), [image[0], image[2]], [(r1, z1_own), (z1, image), (z0, image), (z1_own, q0)])
    spread_faces(SCH1, image)
    t1_faces = total_faces(SCH1, image)
    w1_local = apply_local(t1_faces, l_high, l_low)
    spread_faces(PRE2, w1_local, True)
    gather_forward(2, True)
    w1_local = total_faces(PRE2, w1_local, True)

    def second_step(column):
        rz1 = column(0)
        ratio = rz1 / rz0
        return ratio, rz1 / (column(1) + ratio * (column(2) + column(3)) + ratio * ratio * dq0)

    wide, (ratio, step1) = gather_finish(2, True, second_step)
    w1 = [a + b for a, b in zip(w1_local, wide)]

    t1, w0 = owned(t1_faces), owned(w0)
    for f in range(2):
        place = slice(f * FP, (f + 1) * FP)
        direction = z1_own[f] + ratio * z0_own[f]
        out_ref[0, :, place] = step0 * z0_own[f] + step1 * direction
        out_ref[1, :, place] = r1[f] - step1 * (t1[f] + ratio * q0[f])
        out_ref[2, :, place] = z1_own[f] - step1 * (w1[f] + ratio * w0[f])

    for copy in started:
        copy.wait_send()

    @pl.when(z == 0)
    def _():
        for phase in range(1, 3):
            for s in range(LZ):
                head_copy(phase, s).wait_send()


def unpad(packed_ref, *out_refs):
    for k, out_ref in enumerate(out_refs):
        out_ref[0, 0, :, :F] = packed_ref[k, :, :F]
        out_ref[0, 0, :, F:] = packed_ref[k, :, FP : FP + F]


def shards(applied_loads, bound_block, coupling, interior_inverse, local_inverse, coarse_inverse):
    dma = pltpu.SemaphoreType.DMA
    packed = pl.pallas_call(
        kernel,
        out_shape=jax.ShapeDtypeStruct((3, K, 2 * FP), f32),
        in_specs=[pl.BlockSpec(memory_space=pltpu.HBM)] * 6,
        out_specs=pl.BlockSpec(memory_space=pltpu.VMEM),
        scratch_shapes=[
            pltpu.VMEM((K, 2 * F), f32),
            pltpu.VMEM((NF, NF), f32),
            pltpu.VMEM((NF, NI), f32),
            pltpu.VMEM((NI, NI), f32),
            pltpu.VMEM((NF, NF), f32),
            pltpu.VMEM((32, NC), f32),
            dma((6,)),
            pltpu.VMEM((NP, NP), bf16),
            pltpu.VMEM((NP, NP), bf16),
            pltpu.VMEM((NP, NP), bf16),
            pltpu.VMEM((NP, NP), bf16),
            pltpu.VMEM((2 * NF, NI), bf16),
            pltpu.VMEM((2 * NF, NI), bf16),
            pltpu.VMEM((NF, NF), f32),
            pltpu.VMEM((2, 32, NC // 2), f32),
            pltpu.VMEM((32, NC // 2), f32),
            pltpu.VMEM((LX * LY, 128, 256), bf16),
            pltpu.VMEM((2 * FP, FP), bf16),
            pltpu.VMEM((FP, 3 * FP), bf16),
            pltpu.VMEM((3, LZ, 8, FP), f32),
            pltpu.VMEM((3, 4, FP), f32),
            pltpu.VMEM((3, LZ, 4, FP), f32),
            pltpu.VMEM((3, 8, FP), f32),
            pltpu.VMEM((3, LX * LY, 40, FP), f32),
            pltpu.VMEM((3, 16, FP), f32),
            pltpu.VMEM((3, 5, 16, FP), f32),
            pltpu.VMEM((SLOTS, K, FP), f32),
            pltpu.VMEM((SLOTS, K, FP), f32),
            dma((3, LZ)),
            dma((3, LZ)),
            dma((3, LZ)),
            dma((3, LZ)),
            dma((3, LZ)),
            dma((3,)),
            dma((3, LX * LY)),
            dma((3, LX * LY)),
            dma,
            dma,
            dma((3, 5)),
            dma((3, 5)),
            dma((SLOTS,)),
            dma((SLOTS,)),
        ],
        compiler_params=pltpu.CompilerParams(
            collective_id=0, has_side_effects=True, vmem_limit_bytes=60 * 1024 * 1024
        ),
    )(applied_loads, bound_block, coupling, interior_inverse, local_inverse, coarse_inverse)
    out = jax.ShapeDtypeStruct((1, 1, K, 2 * F), f32)
    return pl.pallas_call(unpad, out_shape=(out, out, out))(packed)


def solution(mesh):
    blocks = P("sx", "sy", None, None)
    return jax.shard_map(
        shards,
        mesh=mesh,
        in_specs=(blocks, blocks, blocks, blocks, blocks, P(("sx", "sy"), None)),
        out_specs=(blocks, blocks, blocks),
        check_vma=False,
    )
```

```python
import jax
import jax.numpy as jnp
from jax import lax
from jax.experimental import pallas as pl
from jax.experimental.pallas import tpu as pltpu
from jax.sharding import PartitionSpec as P

MESH = pl.DeviceIdType.MESH
F = 96
FP = 128
FACES = 4
K = 16
NF = FACES * F
NP = FACES * FP
NI = 1152
NC = 8192
LX, LY, LZ = 4, 4, 8
COLS = 256
LINE_ORDER = sorted(range(LZ), key=lambda s: min(s, LZ - s))
PLANE_ORDER = sorted(range(LX * LY), key=lambda s: min(s // LX, LY - s // LX) + min(s % LX, LX - s % LX))
f32, bf16 = jnp.float32, jnp.bfloat16

LOADS_W, LOADS_N = 0, 1
PRE0, PRE1, PRE2 = 2, 6, 10
SCH0, SCH1 = 12, 16
SLOTS = 20


def split(value):
    high = value.astype(bf16)
    low = (value - high.astype(f32)).astype(bf16)
    return high, low


def dot(left, right):
    return jnp.dot(left, right, preferred_element_type=f32)


def dot_t(left, right):
    return lax.dot_general(left, right, (((1,), (1,)), ((), ())), preferred_element_type=f32)


def transpose_groups(tiles, lane_group):
    a, b, c, d = tiles
    near = lane_group < 2
    a, c = jnp.where(near, a, pltpu.roll(c, 64, 1)), jnp.where(near, pltpu.roll(a, 64, 1), c)
    b, d = jnp.where(near, b, pltpu.roll(d, 64, 1)), jnp.where(near, pltpu.roll(b, 64, 1), d)
    even = lane_group % 2 == 0
    a, b = jnp.where(even, a, pltpu.roll(b, 32, 1)), jnp.where(even, pltpu.roll(a, 96, 1), b)
    c, d = jnp.where(even, c, pltpu.roll(d, 32, 1)), jnp.where(even, pltpu.roll(c, 96, 1), d)
    return a, b, c, d


def pad_split(get_block, high_ref, low_ref):
    high_ref[...] = jnp.zeros_like(high_ref)
    low_ref[...] = jnp.zeros_like(low_ref)
    for a in range(FACES):
        for b in range(FACES):
            high, low = split(get_block(a, b))
            high_ref[a * FP : a * FP + F, b * FP : b * FP + F] = high
            low_ref[a * FP : a * FP + F, b * FP : b * FP + F] = low


def apply_local(faces, high_ref, low_ref):
    high, low = split(jnp.concatenate(faces, axis=1))
    both = dot(jnp.concatenate([high, low], axis=0), high_ref[...])
    result = both[:K] + both[K:] + dot(high, low_ref[...])
    return [result[:, f * FP : (f + 1) * FP] for f in range(FACES)]


def kernel(
    loads_ref, bound_ref, coupling_ref, interior_ref, local_ref, coarse_ref,
    out_ref,
    loads_v, bound_v, coupling_v, interior_v, local_v, coarse_v, load_sem,
    l_high, l_low, s_high, s_low, c_parts, t_parts, schur_v,
    permuted, partner_rows, coarse_w, restrict_v, spread_v,
    line_v, west_out, west_in, head_in, plane_v, part_out, part_in, halo_out, halo_in,
    line_send, line_recv, west_send, west_recv, head_send, head_recv, plane_send, plane_recv,
    swap_send, swap_recv, part_send, part_recv, halo_send, halo_recv,
):
    i = lax.axis_index("sx")
    j = lax.axis_index("sy")
    y, z = lax.div(i, LZ), lax.rem(i, LZ)
    x, core = lax.div(j, 2), lax.rem(j, 2)
    block = y * LX + x
    east = {"sx": i, "sy": lax.rem(j + 1, 2 * LX)}
    west = {"sx": i, "sy": lax.rem(j + 2 * LX - 1, 2 * LX)}
    south = {"sx": lax.rem(i + 1, LY * LZ), "sy": j}
    north = {"sx": lax.rem(i + LY * LZ - 1, LY * LZ), "sy": j}
    partner = {"sx": i, "sy": x * 2 + (1 - core)}
    line = [{"sx": y * LZ + lax.rem(z + s, LZ), "sy": j} for s in range(LZ)]
    west_line = [{"sx": device["sx"], "sy": west["sy"]} for device in line]
    east_line = [{"sx": device["sx"], "sy": east["sy"]} for device in line]
    north_line = [{"sx": lax.rem(y + LY - 1, LY) * LZ + s, "sy": j} for s in range(LZ)]
    south_head = {"sx": lax.rem(y + 1, LY) * LZ, "sy": j}
    plane = [
        {"sx": lax.rem(y + s // LX, LY) * LZ + z, "sy": lax.rem(x + s % LX, LX) * 2 + core} for s in range(LX * LY)
    ]
    south_pair = [south, {"sx": south["sx"], "sy": partner["sy"]}]
    east_pair = [{"sx": i, "sy": lax.rem(x + 1, LX) * 2 + core}, {"sx": i, "sy": lax.rem(x + 1, LX) * 2 + 1 - core}]
    north_other = {"sx": north["sx"], "sy": partner["sy"]}
    west_other = {"sx": i, "sy": lax.rem(x + LX - 1, LX) * 2 + 1 - core}

    fetches = [
        pltpu.make_async_copy(source, target, load_sem.at[k])
        for k, (source, target) in enumerate(
            [
                (loads_ref.at[0, 0], loads_v),
                (coarse_ref, coarse_v),
                (coupling_ref.at[0, 0], coupling_v),
                (interior_ref.at[0, 0], interior_v),
                (local_ref.at[0, 0], local_v),
                (bound_ref.at[0, 0], bound_v),
            ]
        )
    ]
    fetches[0].start()

    barrier = pltpu.get_barrier_semaphore()
    greeted = [device for s in LINE_ORDER[:0:-1] for device in (east_line[s], line[s])]
    greeted += [plane[s] for s in PLANE_ORDER[:0:-1]]
    greeted += [south_head, north_other, west_other, north, south, east_line[0], east, west, partner]
    for device in greeted:
        pl.semaphore_signal(barrier, 1, device_id=device, device_id_type=MESH)

    for fetch in fetches[1:]:
        fetch.start()

    has_west, has_east = j > 0, j < 2 * LX - 1
    has_north, has_south = i > 0, i < LY * LZ - 1

    def halo_copy(slot, device):
        return pltpu.make_async_remote_copy(
            halo_out.at[slot], halo_in.at[slot], halo_send.at[slot], halo_recv.at[slot], device_id=device, device_id_type=MESH
        )

    def halo_start(slot, device, value):
        halo_out[slot] = value
        copy = halo_copy(slot, device)
        copy.start()
        started.append(copy)

    def halo_wait(slot, device, present):
        halo_copy(slot, device).wait_recv()
        return jnp.where(present, halo_in[slot], 0.0)

    started = []

    lane_row = lax.broadcasted_iota(jnp.int32, (1, FP), 1)
    lane_group = lane_row // 32
    south_lanes = lane_row % 32 >= 16
    case = lax.broadcasted_iota(jnp.int32, (K, FP), 0)
    lane = lax.broadcasted_iota(jnp.int32, (K, FP), 1)
    value_lane = lax.broadcasted_iota(jnp.int32, (2 * FP, FP), 0)
    coarse_lane = lax.broadcasted_iota(jnp.int32, (2 * FP, FP), 1) % 32
    in_face = value_lane % FP
    run_of = (value_lane // FP) * 16 + in_face // 6
    restrict_v[...] = ((run_of == coarse_lane) & (in_face < F)).astype(f32).astype(bf16)
    coarse_at = lax.broadcasted_iota(jnp.int32, (FP, 3 * FP), 0)
    value_at = lax.broadcasted_iota(jnp.int32, (FP, 3 * FP), 1)
    value_in = value_at % FP
    face_at = value_at // FP
    first = jnp.where(face_at == 2, (1 - core) * 32, core * 32 + face_at * 16)
    spread_v[...] = ((first + value_in // 6 == coarse_at) & (value_in < F)).astype(f32).astype(bf16)

    def line_copy(phase, s):
        return pltpu.make_async_remote_copy(
            line_v.at[phase, z], line_v.at[phase, z], line_send.at[phase, s], line_recv.at[phase, s],
            device_id=line[s], device_id_type=MESH,
        )

    def west_copy(phase, s):
        return pltpu.make_async_remote_copy(
            west_out.at[phase], west_in.at[phase, z], west_send.at[phase, s], west_recv.at[phase, s],
            device_id=west_line[s], device_id_type=MESH,
        )

    def head_copy(phase, s):
        return pltpu.make_async_remote_copy(
            line_v.at[phase, z], head_in.at[phase], head_send.at[phase, s], head_recv.at[phase],
            device_id=north_line[s], device_id_type=MESH,
        )

    def plane_copy(phase, s):
        rows = pl.ds(0, 40 if phase else 32)
        return pltpu.make_async_remote_copy(
            plane_v.at[phase, block, rows], plane_v.at[phase, block, rows], plane_send.at[phase, s], plane_recv.at[phase, s],
            device_id=plane[s], device_id_type=MESH,
        )

    def part_copy(phase, k, slot, device):
        rows = pl.ds(0, 16 if k == 4 else 8)
        return pltpu.make_async_remote_copy(
            part_out.at[phase, rows], part_in.at[phase, slot, rows], part_send.at[phase, k], part_recv.at[phase, slot],
            device_id=device, device_id_type=MESH,
        )

    def go(copy):
        copy.start()
        started.append(copy)

    def pack(sums):
        packed = sums[:4]
        for q in range(1, 4):
            packed = jnp.where(lane_group == q, sums[4 * q : 4 * q + 4], packed)
        return packed

    def line_start(phase):
        for s in LINE_ORDER[:0:-1]:
            go(line_copy(phase, s))

    def gather_start(phase, own, shared, dots):
        values = [jnp.concatenate(own, axis=1)] + ([jnp.concatenate(shared, axis=1)] if shared else [])
        high, low = split(jnp.concatenate(values, axis=0))
        rows = len(values) * K
        sums = dot(jnp.concatenate([high, low], axis=0), restrict_v[...])
        sums = sums[:rows] + sums[rows:]
        line_v[phase, z, :4] = pack(sums[:K])
        if not shared:
            line_v[phase, z, 4:] = jnp.zeros((4, FP), f32)
        else:
            others = pack(sums[K:])
            west_out[phase] = others
            for s in LINE_ORDER[::-1]:
                go(west_copy(phase, s))
            placed = jnp.zeros((K, FP), f32)
            for d, (left, right) in enumerate(dots):
                product = left[0] * right[0]
                for f in range(1, len(left)):
                    product += left[f] * right[f]
                placed = jnp.where(lane == d * 32 + case, jnp.sum(product, axis=1, keepdims=True), placed)
            row = jnp.sum(placed, axis=0, keepdims=True)
            line_v[phase, z, 4:] = jnp.where(south_lanes, others, row)

            @pl.when(z == 0)
            def _():
                for s in range(LZ):
                    head_copy(phase, s).start()

        if shared:
            line_start(phase)

    def gather_forward(phase, shared):
        for s in range(1, LZ):
            line_copy(phase, s).wait_recv()
        if shared:
            for s in range(LZ):
                west_copy(phase, s).wait_recv()
            head_copy(phase, 0).wait_recv()
        tiles = []
        for s in range(LZ):
            tile = line_v[phase, s, :4]
            if shared:
                if s + 1 < LZ:
                    below = line_v[phase, s + 1, 4:]
                else:
                    below = jnp.where(y < LY - 1, head_in[phase, 4:], 0.0)
                right = jnp.where(has_east, west_in[phase, s], 0.0)
                tile = tile + jnp.where(south_lanes, below, right)
            tiles.append(tile)
        pairs = [jnp.concatenate([tiles[d], tiles[4 + d]], axis=0) for d in range(4)]
        for q, mixed in enumerate(transpose_groups(pairs, lane_group)):
            plane_v[phase, block, 4 * q : 4 * q + 4] = mixed[:4]
            plane_v[phase, block, K + 4 * q : K + 4 * q + 4] = mixed[4:]
        if shared:
            total = line_v[phase, 0]
            for s in range(1, LZ):
                total = total + line_v[phase, s]
            plane_v[phase, block, 2 * K :] = total
        for s in PLANE_ORDER[:0:-1]:
            go(plane_copy(phase, s))

    def gather_finish(phase, last, scalars=None):
        total = jnp.zeros((2 * K, FP), f32)
        sums = jnp.zeros((8, FP), f32)
        for group in (PLANE_ORDER[:5], PLANE_ORDER[5:11], PLANE_ORDER[11:]):
            for s in group:
                if s:
                    plane_copy(phase, s).wait_recv()
            for s in group:
                b = lax.rem(y + LY - s // LX, LY) * LX + lax.rem(x + LX - s % LX, LX)
                value = jnp.concatenate([plane_v[phase, b, :K], plane_v[phase, b, K : 2 * K]], axis=1)
                high, low = split(value)
                total += dot_t(jnp.concatenate([high, low], axis=0), coarse_w[b])
                if phase:
                    sums += plane_v[phase, b, 2 * K :]
        part = total[:K] + total[K:]
        part = part + pltpu.roll(part, 64, 1)
        part = jnp.where(lane_row < 64, part[:8], part[8:])
        part_out[phase, :8] = part
        part_out[phase, 8:] = sums
        if not last:
            for k in range(2):
                go(part_copy(phase, k, 1 + core, south_pair[k]))
                go(part_copy(phase, 2 + k, 3 + core, east_pair[k]))
        go(part_copy(phase, 4, 0, partner))
        part_copy(phase, 4, 0, partner).wait_recv()
        own = part + part_in[phase, 0, :8]
        sums = sums + part_in[phase, 0, 8:]

        def column(d):
            return jnp.sum(jnp.where(lane == d * 32 + case, sums[4:5], 0.0), axis=1, keepdims=True)

        values = scalars(column) if scalars else None
        groups = [own]
        if not last:
            for slot in range(1, 5):
                part_copy(phase, 0, slot, partner).wait_recv()
            groups.append(part_in[phase, 1, :8] + part_in[phase, 2, :8])
            groups.append(jnp.where(core == 0, part_in[phase, 3, :8] + part_in[phase, 4, :8], own))
        high, low = split(jnp.concatenate([half for t in groups for half in (t, pltpu.roll(t, 64, 1))], axis=0))
        rows = len(groups) * K
        wide = dot(jnp.concatenate([high, low], axis=0), spread_v[...])
        wide = wide[:rows] + wide[rows:]
        faces = [wide[:K, :FP], wide[:K, FP : 2 * FP]]
        if not last:
            faces = [wide[2 * K :, 2 * FP :], faces[0], wide[K : 2 * K, FP : 2 * FP], faces[1]]
        return faces, values

    def spread_faces(slot, result, last=False):
        halo_start(slot, west, result[0])
        halo_start(slot + 1, north, result[2])
        if not last:
            halo_start(slot + 2, east, result[1])
            halo_start(slot + 3, south, result[3])

    def total_faces(slot, result, last=False):
        east_total = result[1] + halo_wait(slot, west, has_east)
        south_total = result[3] + halo_wait(slot + 1, north, has_south)
        if last:
            return [east_total, south_total]
        west_total = result[0] + halo_wait(slot + 2, east, has_west)
        north_total = result[2] + halo_wait(slot + 3, south, has_north)
        return inner_faces([west_total, east_total, north_total, south_total])

    def inner_faces(faces):
        return [jnp.where(has_west, faces[0], 0.0), faces[1], jnp.where(has_north, faces[2], 0.0), faces[3]]

    def owned(faces):
        return [faces[1], faces[3]]

    fetches[0].wait()
    padding = jnp.zeros((K, FP - F), f32)
    r0 = [
        jnp.concatenate([loads_v[:, :F], padding], axis=1),
        jnp.concatenate([loads_v[:, F : 2 * F], padding], axis=1),
    ]

    gather_start(0, r0, None, None)

    fetches[1].wait()

    def permute(step, _):
        y_at, rest = lax.div(step, 4), lax.rem(step, 4)
        half, j_half = lax.div(rest, 2), lax.rem(rest, 2)
        tiles = []
        for d in range(4):
            at = ((y_at * LZ + half * 4 + d) * 2 + j_half) * FP
            tiles.append(coarse_v[:, pl.ds(pl.multiple_of(at, FP), FP)])
        for q, mixed in enumerate(transpose_groups(tiles, lane_group)):
            at = (y_at * LX + j_half * 2 + q // 2) * 256 + half * FP
            permuted[q % 2, :, pl.ds(pl.multiple_of(at, FP), FP)] = mixed
        return 0

    lax.fori_loop(0, 16, permute, 0)
    pl.semaphore_wait(barrier, len(greeted) - 1 + LZ * lax.div(LZ - 1 - z, LZ - 1))

    line_start(0)
    halo_start(LOADS_W, east, r0[0])
    halo_start(LOADS_N, south, r0[1])

    swap = pltpu.make_async_remote_copy(
        permuted.at[1 - core], partner_rows, swap_send, swap_recv, device_id=partner, device_id_type=MESH
    )
    go(swap)

    def interior_columns(columns):
        i_high, i_low = split(interior_v[:, columns])
        both = dot(c_parts[...], i_high)
        total = both[:NF] + both[NF:] + dot(c_parts[:NF], i_low)
        t_parts[:NF, columns], t_parts[NF:, columns] = split(total)

    def times_interior(step, _):
        interior_columns(pl.ds(pl.multiple_of(step * COLS, FP), COLS))
        return 0

    fetches[2].wait()
    c_parts[:NF], c_parts[NF:] = split(coupling_v[...])
    fetches[3].wait()
    lax.fori_loop(0, 2, times_interior, 0)

    fetches[4].wait()
    pad_split(lambda a, b: local_v[a * F : (a + 1) * F, b * F : (b + 1) * F], l_high, l_low)
    from_west = halo_wait(LOADS_W, east, has_west)
    from_north = halo_wait(LOADS_N, south, has_north)
    z0_local = apply_local([from_west, r0[0], from_north, r0[1]], l_high, l_low)
    spread_faces(PRE0, z0_local)

    gather_forward(0, False)

    def place_rows(value, at):
        high, low = split(value)
        for b in range(LX * LY):
            coarse_w[b, pl.ds(pl.multiple_of(at, 32), 32)] = high[:, b * 256 : (b + 1) * 256]
            coarse_w[b, pl.ds(pl.multiple_of(64 + at, 32), 32)] = low[:, b * 256 : (b + 1) * 256]

    place_rows(permuted[core], core * 32)
    swap.wait_recv()
    place_rows(partner_rows[...], (1 - core) * 32)
    lax.fori_loop(2, NI // COLS, times_interior, 0)
    interior_columns(slice(NI // COLS * COLS, NI))
    back = dot_t(t_parts[...], c_parts[:NF])
    back = back[:NF] + back[NF:] + dot_t(t_parts[:NF], c_parts[NF:])
    fetches[5].wait()
    schur_v[...] = bound_v[...] - back
    pad_split(lambda a, b: schur_v[a * F : (a + 1) * F, b * F : (b + 1) * F], s_high, s_low)

    z0_local = total_faces(PRE0, z0_local)
    wide, _ = gather_finish(0, False)
    z0 = inner_faces([a + b for a, b in zip(z0_local, wide)])

    image = apply_local(z0, s_high, s_low)
    gather_start(1, owned(image), [image[0], image[2]], [(r0, owned(z0)), (z0, image)])
    spread_faces(SCH0, image)
    q0_faces = total_faces(SCH0, image)
    w0_local = apply_local(q0_faces, l_high, l_low)
    spread_faces(PRE1, w0_local)
    gather_forward(1, True)
    w0_local = total_faces(PRE1, w0_local)

    def first_step(column):
        rz0, dq0 = column(0), column(1)
        return rz0, dq0, rz0 / dq0

    wide, (rz0, dq0, step0) = gather_finish(1, False, first_step)
    w0 = [a + b for a, b in zip(w0_local, wide)]
    z1 = inner_faces([a - step0 * b for a, b in zip(z0, w0)])

    image = apply_local(z1, s_high, s_low)
    q0, z0_own, z1_own = owned(q0_faces), owned(z0), owned(z1)
    r1 = [a - step0 * b for a, b in zip(r0, q0)]
    gather_start(2, owned(image), [image[0], image[2]], [(r1, z1_own), (z1, image), (z0, image), (z1_own, q0)])
    spread_faces(SCH1, image)
    t1_faces = total_faces(SCH1, image)
    w1_local = apply_local(t1_faces, l_high, l_low)
    spread_faces(PRE2, w1_local, True)
    gather_forward(2, True)
    w1_local = total_faces(PRE2, w1_local, True)

    def second_step(column):
        rz1 = column(0)
        ratio = rz1 / rz0
        return ratio, rz1 / (column(1) + ratio * (column(2) + column(3)) + ratio * ratio * dq0)

    wide, (ratio, step1) = gather_finish(2, True, second_step)
    w1 = [a + b for a, b in zip(w1_local, wide)]

    t1, w0 = owned(t1_faces), owned(w0)
    for f in range(2):
        place = slice(f * FP, (f + 1) * FP)
        direction = z1_own[f] + ratio * z0_own[f]
        out_ref[0, :, place] = step0 * z0_own[f] + step1 * direction
        out_ref[1, :, place] = r1[f] - step1 * (t1[f] + ratio * q0[f])
        out_ref[2, :, place] = z1_own[f] - step1 * (w1[f] + ratio * w0[f])

    for copy in started:
        copy.wait_send()

    @pl.when(z == 0)
    def _():
        for phase in range(1, 3):
            for s in range(LZ):
                head_copy(phase, s).wait_send()


def unpad(packed_ref, *out_refs):
    for k, out_ref in enumerate(out_refs):
        out_ref[0, 0, :, :F] = packed_ref[k, :, :F]
        out_ref[0, 0, :, F:] = packed_ref[k, :, FP : FP + F]


def shards(applied_loads, bound_block, coupling, interior_inverse, local_inverse, coarse_inverse):
    dma = pltpu.SemaphoreType.DMA
    packed = pl.pallas_call(
        kernel,
        out_shape=jax.ShapeDtypeStruct((3, K, 2 * FP), f32),
        in_specs=[pl.BlockSpec(memory_space=pltpu.HBM)] * 6,
        out_specs=pl.BlockSpec(memory_space=pltpu.VMEM),
        scratch_shapes=[
            pltpu.VMEM((K, 2 * F), f32),
            pltpu.VMEM((NF, NF), f32),
            pltpu.VMEM((NF, NI), f32),
            pltpu.VMEM((NI, NI), f32),
            pltpu.VMEM((NF, NF), f32),
            pltpu.VMEM((32, NC), f32),
            dma((6,)),
            pltpu.VMEM((NP, NP), bf16),
            pltpu.VMEM((NP, NP), bf16),
            pltpu.VMEM((NP, NP), bf16),
            pltpu.VMEM((NP, NP), bf16),
            pltpu.VMEM((2 * NF, NI), bf16),
            pltpu.VMEM((2 * NF, NI), bf16),
            pltpu.VMEM((NF, NF), f32),
            pltpu.VMEM((2, 32, NC // 2), f32),
            pltpu.VMEM((32, NC // 2), f32),
            pltpu.VMEM((LX * LY, 128, 256), bf16),
            pltpu.VMEM((2 * FP, FP), bf16),
            pltpu.VMEM((FP, 3 * FP), bf16),
            pltpu.VMEM((3, LZ, 8, FP), f32),
            pltpu.VMEM((3, 4, FP), f32),
            pltpu.VMEM((3, LZ, 4, FP), f32),
            pltpu.VMEM((3, 8, FP), f32),
            pltpu.VMEM((3, LX * LY, 40, FP), f32),
            pltpu.VMEM((3, 16, FP), f32),
            pltpu.VMEM((3, 5, 16, FP), f32),
            pltpu.VMEM((SLOTS, K, FP), f32),
            pltpu.VMEM((SLOTS, K, FP), f32),
            dma((3, LZ)),
            dma((3, LZ)),
            dma((3, LZ)),
            dma((3, LZ)),
            dma((3, LZ)),
            dma((3,)),
            dma((3, LX * LY)),
            dma((3, LX * LY)),
            dma,
            dma,
            dma((3, 5)),
            dma((3, 5)),
            dma((SLOTS,)),
            dma((SLOTS,)),
        ],
        compiler_params=pltpu.CompilerParams(
            collective_id=0, has_side_effects=True, vmem_limit_bytes=60 * 1024 * 1024
        ),
    )(applied_loads, bound_block, coupling, interior_inverse, local_inverse, coarse_inverse)
    out = jax.ShapeDtypeStruct((1, 1, K, 2 * F), f32)
    return pl.pallas_call(unpad, out_shape=(out, out, out))(packed)


def solution(mesh):
    blocks = P("sx", "sy", None, None)
    return jax.shard_map(
        shards,
        mesh=mesh,
        in_specs=(blocks, blocks, blocks, blocks, blocks, P(("sx", "sy"), None)),
        out_specs=(blocks, blocks, blocks),
        check_vma=False,
    )
```
